256 devices in a mesh: seq: 32 (over z, y), head: 8 (over x, core).
Axes of the slice: x: 4, y: 4, z: 8, core: 2. Of those that a mesh axis runs over, the one named last changes fastest.
Arguments:
- hidden: bfloat16 [2, 32768, 2048], P(None, 'seq'), may hold values from -6 to 6
- w_qkv: bfloat16 [2048, 2560], P(None, 'head')
- conv_weight: float32 [3, 2560], P(None, 'head'), may hold values from -1 to 1
- norm_gain: bfloat16 [2048], P('head'), may hold values from 0.5 to 1.5
- repo_lengths: int32 [2, 12], replicated, may hold values from 1 to 8192, 32768 in all within a row
Outputs:
- normed: bfloat16 [2, 32768, 2048], P(None, 'seq', 'head')
The draws below stay inside these ranges and needn't reach their ends.
Inputs may be any that keep to these rules, and one draw needn't show every extreme that they name: `repo_lengths`: each row sums to 32768; the longest repository of every sequence has exactly 8192 tokens.
All inputs are finite; a program needn't handle non-finite values.
Results may differ from the reference program's by a relative error of at most 0.0085.
Values may be sent and summed in bfloat16 or wider, within the bound.
A program may use at most 128 MiB of HBM per device.

```python
import math
import jax
import jax.numpy as jnp
import numpy as np
from jax import lax

D = 2048
H = 16
FEAT = 16
HEAD = 128
KERNEL = 3
NSEG = 12
SEQS = 2
PHI = 273
LEN = 32768


def draw_w_qkv(key, part):
    width = 2 * FEAT + HEAD
    columns = H * width
    key_one, key_two = jax.random.split(key)
    column = jnp.arange(columns)
    head_of = (column // width).astype(jnp.float32)
    is_value = column % width >= 2 * FEAT
    base = 3.0
    entries = jax.random.normal(key_one, (D, columns), jnp.float32)
    jitter = jnp.exp(jax.random.uniform(key_two, (columns,), jnp.float32, -0.693, 0.693))
    rising = jnp.exp(jnp.log(base) * head_of / (H - 1))
    scale = jnp.where(is_value, rising * jitter, 1.0)
    return (entries * scale[None, :] / jnp.sqrt(jnp.float32(D))).astype(jnp.bfloat16)


def block_levels(stream_key, shape, shards, low, largest):
    level = 1.0
    for position, parts in shards:
        draws = jax.random.uniform(jax.random.fold_in(jax.random.fold_in(stream_key, 6), position), (parts,), jnp.float32, low / len(shards), largest / len(shards))
        level = level * jnp.repeat(jnp.exp(draws), shape[position] // parts).reshape((-1,) + (1,) * (len(shape) - 1 - position))
    return level


def profile(amount, total, reach, slope):
    weights = [(1 << 20) // math.isqrt(standing ** slope) + 1 for standing in range(2, amount + 1)]
    rest, holding = total - reach - (amount - 1), [1] * (amount - 1)
    while rest > 0:
        movable = [i for i in range(amount - 1) if holding[i] < reach]
        mass, remaining = sum([weights[i] for i in movable]), rest
        for i in movable:
            addition = min(reach - holding[i], max(1, remaining * weights[i] // mass), rest)
            holding[i] = holding[i] + addition
            rest = rest - addition
    return np.array([reach] + holding)


def uneven_parts(rng, amount, total, bound, slope):
    if amount == 2:
        one = jax.random.randint(rng, (), max(1, total - bound), min(bound, total - 1) + 1)
        return jnp.stack([one, total - one])
    sizes = jnp.asarray(profile(amount, total, bound, slope), jnp.int32)
    twos = (amount - 1) // 2
    giver, receiver = sizes[1:1 + 2 * twos:2], sizes[2:2 + 2 * twos:2]
    slack = jnp.minimum(giver - 1, bound - receiver)
    moved = jax.random.randint(jax.random.fold_in(rng, 1), (twos,), 0, 1 << 20) % (slack + 1)
    sizes = sizes.at[1:1 + 2 * twos:2].set(giver - moved).at[2:2 + 2 * twos:2].set(receiver + moved)
    return sizes[jax.random.permutation(jax.random.fold_in(rng, 2), amount)]


def bell_draw(key, dims, scale, most, pieces=(), kind=jnp.bfloat16):
    array = jax.random.normal(key, dims, jnp.float32) * scale
    if len(pieces) > 0:
        array = block_levels(key, dims, pieces, -0.22, 0.18) * array
    return jnp.clip(array, min=-most, max=most).astype(kind)


def setup_inputs(seed: int = 0) -> dict:
    seeds = jax.random.split(jax.random.key(seed), 6)
    return {
        "hidden": bell_draw(seeds[0], (SEQS, LEN, D), 1.0, 6.0, ((1, 32),)),
        "w_qkv": draw_w_qkv(jax.random.fold_in(seeds[5], 71), 0),
        "conv_weight": jnp.clip(jax.random.uniform(seeds[2], (KERNEL, H * (2 * FEAT + HEAD)), jnp.float32, -1.0, 1.0) * block_levels(seeds[2], (KERNEL, H * (2 * FEAT + HEAD)), ((1, 8),), -0.4, 0.0), -1.0, 1.0),
        "norm_gain": jnp.clip(1.0 + 0.1 * jax.random.normal(seeds[3], (H * HEAD,), jnp.float32), 0.5, 1.5).astype(jnp.bfloat16),
        "repo_lengths": jax.vmap(lambda own: uneven_parts(own, NSEG, LEN, LEN // 4, 2))(jax.random.split(seeds[4], SEQS)).reshape((SEQS, NSEG)).astype(jnp.int32),
    }


def features(values):
    first = values * FEAT ** (-0.25)
    outer = (values[..., :, None] * values[..., None, :]).reshape(values.shape[:-1] + (FEAT * FEAT,))
    outer = outer * (1.0 / (2.0 * FEAT) ** 0.5)
    ones = jnp.ones(values.shape[:-1] + (1,), values.dtype)
    return jnp.concatenate([ones, first, outer], axis=-1)

def attend_head(phi_query, phi_key, values, segment):
    block_rows = min(256, LEN)
    count = LEN // block_rows
    blocks = (phi_query.reshape(count, block_rows, PHI), phi_key.reshape(count, block_rows, PHI), values.reshape(count, block_rows, HEAD), segment.reshape(count, block_rows))
    order = jnp.arange(block_rows, dtype=jnp.int32)
    causal = order[:, None] >= order[None, :]

    def advance(carry, block):
        state, norm, last_seg = carry
        query_block, key_block, value_block, seg_block = block
        scores = jnp.dot(query_block, key_block.T, preferred_element_type=jnp.float32)
        scores = jnp.where(causal & (seg_block[:, None] == seg_block[None, :]), scores, 0.0)
        numer = jnp.dot(scores.astype(jnp.bfloat16), value_block, preferred_element_type=jnp.float32)
        denom = lax.optimization_barrier(jnp.sum(scores, axis=1))
        use_carry = seg_block == last_seg
        query_wide = query_block.astype(jnp.float32)
        numer = numer + jnp.where(use_carry[:, None], jnp.dot(query_wide, state, precision=lax.Precision.HIGHEST), 0.0)
        denom = denom + jnp.where(use_carry, jnp.dot(query_wide, norm, precision=lax.Precision.HIGHEST), 0.0)
        tail_seg = seg_block[-1].astype(jnp.int32)
        inside = seg_block == tail_seg
        masked = jnp.where(inside[:, None], key_block, jnp.zeros_like(key_block))
        add_state = jnp.dot(masked.T, value_block, preferred_element_type=jnp.float32)
        add_norm = lax.optimization_barrier(jnp.sum(masked.astype(jnp.float32), axis=0))
        keep_old = tail_seg == last_seg
        state = add_state + jnp.where(keep_old, state, jnp.float32(0.0))
        norm = add_norm + jnp.where(keep_old, norm, jnp.float32(0.0))
        return ((state.astype(jnp.float32), norm.astype(jnp.float32), tail_seg), numer / denom[:, None])
    start_carry = (jnp.zeros((PHI, HEAD), jnp.float32), jnp.zeros((PHI,), jnp.float32), jnp.int32(-1))
    _, results = lax.scan(advance, start_carry, blocks)
    return results.reshape(LEN, HEAD)

def one_sequence(packed):
    phi_query, phi_key, values, segment = packed
    return jax.vmap(attend_head, in_axes=(1, 1, 1, None), out_axes=1)(phi_query, phi_key, values, segment)

def reference(hidden, w_qkv, conv_weight, norm_gain, repo_lengths):
    width = 2 * FEAT + HEAD
    qkv = jnp.dot(hidden.reshape(SEQS * LEN, D), w_qkv, preferred_element_type=jnp.float32)
    qkv = qkv.astype(jnp.bfloat16).reshape(SEQS, LEN, H * width)
    starts = (jnp.cumsum(repo_lengths, axis=1) - repo_lengths).astype(jnp.int32)
    places = jnp.arange(LEN, dtype=jnp.int32)
    segment = (lax.optimization_barrier(jnp.sum((starts[:, None, :] <= places[None, :, None]).astype(jnp.int32), axis=2)) - 1).astype(jnp.int32)
    field = qkv.astype(jnp.float32)
    mixed = conv_weight[0] * field
    for back in range(1, KERNEL):
        shifted = jnp.pad(field, ((0, 0), (back, 0), (0, 0)))[:, :LEN]
        seg_back = jnp.pad(segment, ((0, 0), (back, 0)), constant_values=-1)[:, :LEN]
        mixed = mixed + conv_weight[back] * jnp.where((seg_back == segment)[..., None], shifted, 0.0)
    mixed = mixed.astype(jnp.bfloat16).reshape(SEQS, LEN, H, width)
    phi_query = features(mixed[..., :FEAT].astype(jnp.float32)).astype(jnp.bfloat16)
    phi_key = features(mixed[..., FEAT:2 * FEAT].astype(jnp.float32)).astype(jnp.bfloat16)
    values = mixed[..., 2 * FEAT:]
    attn = lax.map(one_sequence, (phi_query, phi_key, values, segment))
    attn = attn.reshape(SEQS, LEN, H * HEAD)
    mean_sq = lax.optimization_barrier(jnp.mean(attn * attn, axis=-1))
    scaled = attn * lax.rsqrt(mean_sq + 1e-06)[..., None] * norm_gain.astype(jnp.float32)
    return scaled.astype(jnp.bfloat16)
```

```python
import functools
import jax
import jax.numpy as jnp
import numpy as np
from jax import lax
from jax.experimental import pallas as pl
from jax.experimental.pallas import tpu as pltpu
from jax.sharding import PartitionSpec as P

FEAT = 16
HEAD = 128
WIDTH = 2 * FEAT + HEAD
NSEG = 12
ROW = 4
CHUNK = 256
RIM = 16
KEPT = 160
PIECE = 80
ONE = 64
ZROW = 153
MESH = pl.DeviceIdType.MESH
bf16 = jnp.bfloat16
f32 = jnp.float32


def tables():
    pairs = [(0, i) for i in range(FEAT + 1)]
    pairs += [(i, j) for i in range(1, FEAT + 1) for j in range(i, FEAT + 1)]
    query = np.zeros((2, 128, 512), np.float32)
    key = np.zeros((2, 2 * KEPT, 128), np.float32)
    move = np.zeros((2, 128, 128), np.float32)
    for h in range(2):
        def lane(i, base):
            return ONE if i == 0 else base + i - 1
        qb, kb = 32 * h, 32 * h + FEAT
        for f, (i, j) in enumerate(pairs):
            if j == 0:
                sq, sk = 1.0, 1 / 8
            elif i == 0:
                sq, sk = 1 / 4, 1 / 8
            elif i == j:
                sq, sk = 1 / 16, 1 / 16
            else:
                sq, sk = 1 / 8, 1 / 16
            query[h, lane(i, qb), f] = sq
            query[h, lane(j, qb), 256 + f] = 1.0
            key[h, f, lane(i, kb)] = sk
            key[h, KEPT + f, lane(j, kb)] = 1.0
        for i in range(FEAT):
            move[h, kb + i, qb + i] = 1 / 16
        move[h, ONE, ONE] = 1 / 4
    return query.astype(jnp.bfloat16), key.astype(jnp.bfloat16), move.astype(jnp.bfloat16)


def nt(a, b):
    return lax.dot_general(a, b, (((1,), (1,)), ((), ())), preferred_element_type=f32)


def nn(a, b):
    return jnp.dot(a, b, preferred_element_type=f32)


def iota(shape, dim):
    return lax.broadcasted_iota(jnp.int32, shape, dim)


def kernel(zn, hn, hid, wq, conv, gain, lengths, eq, ek, mk, out,
           hbuf, wraw, wbuf, taps, qkv, lo, qk, kk, vv, phq, nd, att, rim_s, rim_r, lbuf, xbuf, rsend, zbuf,
           esend, ebuf, ssb, ssr, obuf,
           wsem, hsem, osem, rim_sem, p1s, p1r, p2s, p2r, p3s, p3r, sss, ssrs):
    T = hbuf.shape[1]
    C = T // CHUNK
    G = T // 128
    me = lax.axis_index("seq")
    hd = lax.axis_index("head")
    z = me // ROW
    y = lax.rem(me, ROW)

    def at_seq(i):
        return (i, hd)

    def along_y(k):
        return (z * ROW + lax.rem(y + k + ROW, ROW), hd)

    def along_z(k):
        return (lax.rem(z + k + zn, zn) * ROW + y, hd)

    def along_h(k):
        return (me, lax.rem(hd + k + hn, hn))

    nxt = at_seq(lax.rem(me + 1, zn * ROW))
    prv = at_seq(lax.rem(me + zn * ROW - 1, zn * ROW))

    wcopy = pltpu.make_async_copy(wq, wraw, wsem)
    wcopy.start()
    order = [(0, C - 1), (1, C - 1)] + [(0, c) for c in range(C - 1)] + [(1, c) for c in range(C - 1)]

    def fetch(s, c):
        rows = pl.ds(c * CHUNK, CHUNK)
        return pltpu.make_async_copy(hid.at[s, rows], hbuf.at[s, rows], hsem.at[s, c])

    for s, c in order:
        fetch(s, c).start()

    barrier = pltpu.get_barrier_semaphore()
    sources = [prv] + [along_y(-k) for k in (1, 2, 3)] + [along_z(-k) for k in (1, 2)]
    sources += [along_h(-k) for k in range(1, hn)]
    for d in sources:
        pl.semaphore_signal(barrier, inc=1, device_id=d, device_id_type=MESH)

    starts = []
    for s in range(2):
        run = jnp.int32(0)
        own = []
        for r in range(NSEG - 1):
            run = run + lengths[s, r]
            own.append(run)
        starts.append(own)

    def begin_of(s, t):
        found = jnp.int32(0)
        for b in starts[s]:
            found = jnp.where(b <= t, b, found)
        return found

    base = me * T

    for s in range(2):
        for r0 in range(0, T, 64):
            pos = base + r0 + iota((64, 128), 0)
            found = jnp.zeros((64, 128), jnp.int32)
            for b in starts[s]:
                found = jnp.where(pos >= b, b, found)
            lo[s, r0:r0 + 64, :] = found - base
        for h in range(2):
            vv[2 * s + h, :, HEAD:] = jnp.ones((T, HEAD), bf16)

    for j in range(3):
        row = conv[j:j + 1, :]
        taps[j:j + 1, 0:128] = row[:, 32:160]
        taps[j:j + 1, 128:256] = row[:, 192:320]
        taps[j:j + 1, 256:384] = jnp.concatenate(
            [row[:, 0:32], row[:, 160:192], jnp.zeros((1, 64), f32)], axis=1)

    wcopy.wait()
    D = wraw.shape[0]
    for r0 in range(0, D, 256):
        rows = slice(r0, r0 + 256)
        wbuf[rows, 0:128] = wraw[rows, 32:160]
        wbuf[rows, 128:256] = wraw[rows, 192:320]
        wbuf[rows, 256:384] = jnp.concatenate(
            [wraw[rows, 0:32], wraw[rows, 160:192], jnp.zeros((256, 64), bf16)], axis=1)

    def project(s, c):
        fetch(s, c).wait()
        low = nn(hbuf[s, c * CHUNK:(c + 1) * CHUNK, :], wbuf[...]).astype(bf16)
        qkv[s, RIM + c * CHUNK:RIM + (c + 1) * CHUNK, :] = low.astype(f32)
        if c == C - 1:
            rim_s[s] = low[CHUNK - RIM:, :]

    rim = pltpu.make_async_remote_copy(rim_s, rim_r, rim_sem.at[0], rim_sem.at[1], device_id=nxt, device_id_type=MESH)

    def mix(s, c):
        for r0 in range(c * CHUNK, (c + 1) * CHUNK, 64):
            first = lo[s, r0:r0 + 64, :]
            pos = r0 + iota((64, 128), 0)
            one_back = first < pos
            two_back = first < pos - 1
            for j in range(3):
                lanes = slice(128 * j, 128 * j + 128)
                x0 = qkv[s, RIM + r0:RIM + r0 + 64, lanes]
                x1 = qkv[s, RIM + r0 - 1:RIM + r0 + 63, lanes]
                x2 = qkv[s, RIM + r0 - 2:RIM + r0 + 62, lanes]
                m = taps[0:1, lanes] * x0
                m = m + taps[1:2, lanes] * jnp.where(one_back, x1, 0.0)
                m = m + taps[2:3, lanes] * jnp.where(two_back, x2, 0.0)
                if j < 2:
                    vv[2 * s + j, r0:r0 + 64, 0:HEAD] = m.astype(bf16)
                else:
                    m = jnp.where(iota((64, 128), 1) == ONE, 1.0, m)
                    qk[s, r0:r0 + 64, :] = m.astype(bf16)

    def summarise(s, h):
        g = 2 * s + h
        inside = begin_of(s, base + T - 1) - base
        total = jnp.zeros((KEPT, 2 * HEAD), f32)
        for c in range(C):
            rows = slice(c * CHUNK, (c + 1) * CHUNK)
            wide = nt(ek[h], qk[s, rows, :])
            phi = wide[:KEPT] * wide[KEPT:]
            phi = jnp.where(c * CHUNK + iota((KEPT, CHUNK), 1) >= inside, phi, 0.0).astype(bf16)
            total = total + nn(phi, vv[g, rows, :])
        state, norm = total[:, :HEAD], total[:, HEAD:]
        f, l = iota((KEPT, HEAD), 0), iota((KEPT, HEAD), 1)
        n0 = jnp.sum(jnp.where(f == l, norm, 0.0), axis=0, keepdims=True)
        n1 = jnp.sum(jnp.where(f == l + HEAD, norm, 0.0), axis=0, keepdims=True)
        state = jnp.where(f == ZROW, n0, jnp.where(f == ZROW + 1, n1, state)).astype(bf16)
        lbuf[s, 2 * h] = state[:PIECE]
        lbuf[s, 2 * h + 1] = state[PIECE:]

    def p1(s, k):
        return pltpu.make_async_remote_copy(
            lbuf.at[s, lax.rem(y + k, ROW)], xbuf.at[s, k - 1], p1s.at[s, k - 1], p1r.at[s, k - 1],
            device_id=along_y(k), device_id_type=MESH)

    def p2(s, k):
        return pltpu.make_async_remote_copy(
            rsend.at[s], zbuf.at[s, k - 1], p2s.at[s, k - 1], p2r.at[s, k - 1],
            device_id=along_z(k), device_id_type=MESH)

    def p3(s, k):
        return pltpu.make_async_remote_copy(
            esend.at[s, k - 1], ebuf.at[s, y], p3s.at[s, k - 1], p3r.at[s, k - 1],
            device_id=along_y(k), device_id_type=MESH)

    def p3_in(s, k):
        return pltpu.make_async_remote_copy(
            esend.at[s, k - 1], ebuf.at[s, lax.rem(y - k + ROW, ROW)], p3s.at[s, k - 1], p3r.at[s, k - 1],
            device_id=along_y(k), device_id_type=MESH)

    def ss(s, k):
        return pltpu.make_async_remote_copy(
            ssb.at[s], ssr.at[s, k - 1], sss.at[s, k - 1], ssrs.at[s, k - 1],
            device_id=along_h(k), device_id_type=MESH)

    rowbase = z * (ROW * T)

    def last_of(j):
        return rowbase + (j + 1) * T - 1

    def gathered(s):
        parts = [lbuf[s, y].astype(f32)]
        places = [y]
        for k in (1, 2, 3):
            parts.append(xbuf[s, k - 1].astype(f32))
            places.append(lax.rem(y - k + ROW, ROW))
        return parts, places

    def row_sum(s):
        for k in (1, 2, 3):
            p1(s, k).wait_recv()
        parts, places = gathered(s)
        begin = begin_of(s, last_of(ROW - 1))
        total = jnp.zeros((PIECE, HEAD), f32)
        for part, j in zip(parts, places):
            total = total + jnp.where(begin <= last_of(j), part, 0.0)
        rsend[s] = total.astype(bf16)
        for k in (1, 2):
            p2(s, k).start()

    def entering(s):
        for k in (1, 2):
            p2(s, k).wait_recv()
        parts, places = gathered(s)
        one, two = zbuf[s, 0].astype(f32), zbuf[s, 1].astype(f32)
        for k in (1, 2, 3, 0):
            target = lax.rem(y + k, ROW)
            begin = begin_of(s, rowbase + target * T)
            total = jnp.where(begin < rowbase, one, 0.0) + jnp.where(begin < rowbase - ROW * T, two, 0.0)
            for part, j in zip(parts, places):
                reach = jnp.where(j < target, last_of(j), -1)
                total = total + jnp.where(begin <= reach, part, 0.0)
            if k:
                esend[s, k - 1] = total.astype(bf16)
                p3(s, k).start()
            else:
                ebuf[s, y] = total.astype(bf16)

    def attend(s, h):
        g = 2 * s + h
        for c in range(C):
            rows = slice(c * CHUNK, (c + 1) * CHUNK)
            q = qk[s, rows, :]
            first = jnp.concatenate([lo[s, rows, :]] * (CHUNK // 128), axis=1)
            cols = iota((CHUNK, CHUNK), 1)
            parts = []
            for b in range(c + 1):
                u = nt(q, kk[g, b * CHUNK:(b + 1) * CHUNK, :])
                u = u * u + 0.0625
                keep = cols + b * CHUNK >= first
                if b == c:
                    keep = keep & (cols <= iota((CHUNK, CHUNK), 0))
                parts.append(jnp.where(keep, u, 0.0).astype(bf16))
            weights = parts[0] if c == 0 else jnp.concatenate(parts, axis=1)
            nd[g, rows, :] = nn(weights, vv[g, :(c + 1) * CHUNK, :])

    def queries(s, h):
        g = 2 * s + h
        for c in range(C):
            rows = slice(c * CHUNK, (c + 1) * CHUNK)
            ab = nn(qk[s, rows, :], eq[h])
            phq[g, rows, :] = (ab[:, :256] * ab[:, 256:]).astype(bf16)

    def keys(s, h):
        for c in range(C):
            rows = slice(c * CHUNK, (c + 1) * CHUNK)
            kk[2 * s + h, rows, :] = nn(qk[s, rows, :], mk[h]).astype(bf16)

    def finish(s):
        for k in (1, 2, 3):
            p3_in(s, k).wait_recv()
        rhs = []
        f, l = iota((KEPT, HEAD), 0), iota((KEPT, HEAD), 1)
        for h in range(2):
            state = jnp.concatenate([ebuf[s, 2 * h], ebuf[s, 2 * h + 1]], axis=0)
            wide = state.astype(f32)
            n0, n1 = wide[ZROW:ZROW + 1], wide[ZROW + 1:ZROW + 2]
            norm = jnp.sum(jnp.where(f == l, n0, 0.0) + jnp.where(f == l + HEAD, n1, 0.0), axis=1, keepdims=True)
            norm = jnp.broadcast_to(norm, (KEPT, HEAD)).astype(bf16)
            both = jnp.concatenate([state, norm], axis=1)
            rhs.append(jnp.concatenate([both, jnp.zeros((256 - KEPT, 256), bf16)], axis=0))
        eye = iota((128, 128), 0) == iota((128, 128), 1)
        for r0 in range(0, T, 128):
            rows = slice(r0, r0 + 128)
            use = lo[s, rows, :] < 0
            squares = jnp.zeros((128, 128), f32)
            for h in range(2):
                g = 2 * s + h
                came = nn(phq[g, rows, :], rhs[h])
                num = nd[g, rows, :HEAD] + jnp.where(use, came[:, :HEAD], 0.0)
                den = nd[g, rows, HEAD:] + jnp.where(use, came[:, HEAD:], 0.0)
                a = num / den
                att[s, rows, h * HEAD:(h + 1) * HEAD] = a
                squares = squares + a * a
            col = jnp.sum(squares, axis=1, keepdims=True)
            i = r0 // 128
            ssb[s, i:i + 1, :] = jnp.sum(jnp.where(eye, col, 0.0), axis=0, keepdims=True)
        for k in range(1, hn):
            ss(s, k).start()

    def write(s, c):
        rows = pl.ds(c * CHUNK, CHUNK)
        return pltpu.make_async_copy(obuf.at[s, rows], out.at[s, rows], osem.at[s, c])

    def scale(s):
        for k in range(1, hn):
            ss(s, k).wait_recv()
        total = ssb[s]
        for k in range(1, hn):
            total = total + ssr[s, k - 1]
        factor = lax.rsqrt(total / (hn * 2 * HEAD) + 1e-06)
        eye = iota((128, 128), 0) == iota((128, 128), 1)
        g = gain[...].astype(f32)
        for r0 in range(0, T, 128):
            i = r0 // 128
            rows = slice(r0, r0 + 128)
            col = jnp.sum(jnp.where(eye, factor[i:i + 1, :], 0.0), axis=1, keepdims=True)
            obuf[s, rows, :] = (att[s, rows, :] * col * g).astype(bf16)
            if (r0 + 128) % CHUNK == 0:
                write(s, r0 // CHUNK).start()

    project(0, C - 1)
    project(1, C - 1)
    pl.semaphore_wait(barrier, len(sources))
    rim.start()
    for c in range(C - 1):
        project(0, c)
    for c in range(1, C):
        mix(0, c)
    rim.wait_recv()
    for s in range(2):
        qkv[s, 0:RIM, :] = rim_r[s].astype(f32)
    mix(0, 0)
    for h in range(2):
        summarise(0, h)
    for k in (1, 2, 3):
        p1(0, k).start()
    for c in range(C - 1):
        project(1, c)
    for c in range(C):
        mix(1, c)
    for h in range(2):
        summarise(1, h)
    for k in (1, 2, 3):
        p1(1, k).start()
    row_sum(0)
    keys(0, 0)
    attend(0, 0)
    row_sum(1)
    keys(0, 1)
    attend(0, 1)
    entering(0)
    queries(0, 0)
    queries(0, 1)
    keys(1, 0)
    attend(1, 0)
    entering(1)
    queries(1, 0)
    queries(1, 1)
    keys(1, 1)
    attend(1, 1)
    finish(0)
    finish(1)
    scale(0)
    scale(1)
    for s in range(2):
        for c in range(C):
            write(s, c).wait()
    rim.wait_send()
    for s in range(2):
        for k in (1, 2, 3):
            p1(s, k).wait_send()
            p3(s, k).wait_send()
        for k in (1, 2):
            p2(s, k).wait_send()
        for k in range(1, hn):
            ss(s, k).wait_send()


def shards(zn, hn, hidden, w_qkv, conv_weight, norm_gain, repo_lengths):
    seqs, T, D = hidden.shape
    C = T // CHUNK
    query, key, move = tables()
    any_spec = pl.BlockSpec(memory_space=pl.ANY)
    vmem = pl.BlockSpec(memory_space=pltpu.VMEM)
    dma = pltpu.SemaphoreType.DMA
    return pl.pallas_call(
        functools.partial(kernel, zn, hn),
        out_shape=jax.ShapeDtypeStruct((seqs, T, 2 * HEAD), bf16),
        in_specs=[any_spec, any_spec, vmem, vmem, pl.BlockSpec(memory_space=pltpu.SMEM), vmem, vmem, vmem],
        out_specs=any_spec,
        scratch_shapes=[
            pltpu.VMEM((2, T, D), bf16),
            pltpu.VMEM((D, 2 * WIDTH), bf16),
            pltpu.VMEM((D, 384), bf16),
            pltpu.VMEM((8, 384), f32),
            pltpu.VMEM((2, RIM + T, 384), f32),
            pltpu.VMEM((2, T, 128), jnp.int32),
            pltpu.VMEM((2, T, 128), bf16),
            pltpu.VMEM((4, T, 128), bf16),
            pltpu.VMEM((4, T, 256), bf16),
            pltpu.VMEM((4, T, 256), bf16),
            pltpu.VMEM((4, T, 256), f32),
            pltpu.VMEM((2, T, 256), f32),
            pltpu.VMEM((2, RIM, 384), bf16),
            pltpu.VMEM((2, RIM, 384), bf16),
            pltpu.VMEM((2, ROW, PIECE, HEAD), bf16),
            pltpu.VMEM((2, 3, PIECE, HEAD), bf16),
            pltpu.VMEM((2, PIECE, HEAD), bf16),
            pltpu.VMEM((2, 2, PIECE, HEAD), bf16),
            pltpu.VMEM((2, 3, PIECE, HEAD), bf16),
            pltpu.VMEM((2, ROW, PIECE, HEAD), bf16),
            pltpu.VMEM((2, T // 128, 128), f32),
            pltpu.VMEM((2, max(hn - 1, 1), T // 128, 128), f32),
            pltpu.VMEM((2, T, 256), bf16),
            dma,
            dma((2, C)),
            dma((2, C)),
            dma((2,)),
            dma((2, 3)),
            dma((2, 3)),
            dma((2, 2)),
            dma((2, 2)),
            dma((2, 3)),
            dma((2, 3)),
            dma((2, max(hn - 1, 1))),
            dma((2, max(hn - 1, 1))),
        ],
        compiler_params=pltpu.CompilerParams(
            collective_id=0, has_side_effects=True, vmem_limit_bytes=60 * 1024 * 1024),
        name="packed_linear_attention",
    )(hidden, w_qkv, conv_weight, norm_gain.reshape(1, 2 * HEAD), repo_lengths,
      jnp.asarray(query), jnp.asarray(key), jnp.asarray(move))


def solution(mesh):
    zn, hn = mesh.shape["seq"] // ROW, mesh.shape["head"]
    in_specs = (P(None, "seq", None), P(None, "head"), P(None, "head"), P("head"), P())
    out_specs = P(None, "seq", "head")
    return jax.shard_map(
        functools.partial(shards, zn, hn), mesh=mesh, in_specs=in_specs, out_specs=out_specs, check_vma=False)
```

```python
import functools
import jax
import jax.numpy as jnp
import numpy as np
from jax import lax
from jax.experimental import pallas as pl
from jax.experimental.pallas import tpu as pltpu
from jax.sharding import PartitionSpec as P

FEAT = 16
HEAD = 128
WIDTH = 2 * FEAT + HEAD
NSEG = 12
ROW = 4
CHUNK = 256
RIM = 16
KEPT = 160
PIECE = 80
ONE = 64
ZROW = 153
MESH = pl.DeviceIdType.MESH
bf16 = jnp.bfloat16
f32 = jnp.float32


def tables():
    pairs = [(0, i) for i in range(FEAT + 1)]
    pairs += [(i, j) for i in range(1, FEAT + 1) for j in range(i, FEAT + 1)]
    query = np.zeros((2, 128, 512), np.float32)
    key = np.zeros((2, 2 * KEPT, 128), np.float32)
    move = np.zeros((2, 128, 128), np.float32)
    for h in range(2):
        def lane(i, base):
            return ONE if i == 0 else base + i - 1
        qb, kb = 32 * h, 32 * h + FEAT
        for f, (i, j) in enumerate(pairs):
            if j == 0:
                sq, sk = 1.0, 1 / 8
            elif i == 0:
                sq, sk = 1 / 4, 1 / 8
            elif i == j:
                sq, sk = 1 / 16, 1 / 16
            else:
                sq, sk = 1 / 8, 1 / 16
            query[h, lane(i, qb), f] = sq
            query[h, lane(j, qb), 256 + f] = 1.0
            key[h, f, lane(i, kb)] = sk
            key[h, KEPT + f, lane(j, kb)] = 1.0
        for i in range(FEAT):
            move[h, kb + i, qb + i] = 1 / 16
        move[h, ONE, ONE] = 1 / 4
    return query.astype(jnp.bfloat16), key.astype(jnp.bfloat16), move.astype(jnp.bfloat16)


def nt(a, b):
    return lax.dot_general(a, b, (((1,), (1,)), ((), ())), preferred_element_type=f32)


def nn(a, b):
    return jnp.dot(a, b, preferred_element_type=f32)


def iota(shape, dim):
    return lax.broadcasted_iota(jnp.int32, shape, dim)


def kernel(zn, hn, hid, wq, conv_in, gain_in, lengths, eq_in, ek_in, mk_in, out,
           hbuf, wbuf, conv, gain, eq, ek, mk, taps, qkv, lo, qk, kk, vv, phq, nd, att, rim_s, rim_r, lbuf, xbuf, rsend, zbuf,
           esend, ebuf, ssb, ssr, obuf,
           wsem, csem, hsem, osem, rim_sem, p1s, p1r, p2s, p2r, p3s, p3r, sss, ssrs):
    T = hbuf.shape[1]
    C = T // CHUNK
    G = T // 128
    me = lax.axis_index("seq")
    hd = lax.axis_index("head")
    z = me // ROW
    y = lax.rem(me, ROW)

    def at_seq(i):
        return (i, hd)

    def along_y(k):
        return (z * ROW + lax.rem(y + k + ROW, ROW), hd)

    def along_z(k):
        return (lax.rem(z + k + zn, zn) * ROW + y, hd)

    def along_h(k):
        return (me, lax.rem(hd + k + hn, hn))

    nxt = at_seq(lax.rem(me + 1, zn * ROW))
    prv = at_seq(lax.rem(me + zn * ROW - 1, zn * ROW))

    def columns(i):
        source, target, many = ((32, 0, 128), (192, 128, 128), (0, 256, 32), (160, 288, 32))[i]
        return pltpu.make_async_copy(wq.at[pl.ds(source, many)], wbuf.at[pl.ds(target, many)], wsem.at[i])

    def small(i):
        source, target = ((conv_in, conv), (gain_in, gain), (ek_in, ek), (mk_in, mk), (eq_in, eq))[i]
        return pltpu.make_async_copy(source, target, csem.at[i])

    for i in range(4):
        columns(i).start()
    order = [(0, C - 1), (1, C - 1)] + [(0, c) for c in range(C - 1)] + [(1, c) for c in range(C - 1)]

    def fetch(s, c):
        rows = pl.ds(c * CHUNK, CHUNK)
        return pltpu.make_async_copy(hid.at[s, rows], hbuf.at[s, rows], hsem.at[s, c])

    for n, (s, c) in enumerate(order):
        fetch(s, c).start()
        if n == 1:
            for i in range(5):
                small(i).start()

    barrier = pltpu.get_barrier_semaphore()
    sources = [prv] + [along_y(-k) for k in (1, 2, 3)] + [along_z(-k) for k in (1, 2)]
    sources += [along_h(-k) for k in range(1, hn)]
    for d in sources:
        pl.semaphore_signal(barrier, inc=1, device_id=d, device_id_type=MESH)

    starts = []
    for s in range(2):
        run = jnp.int32(0)
        own = []
        for r in range(NSEG - 1):
            run = run + lengths[s, r]
            own.append(run)
        starts.append(own)

    def begin_of(s, t):
        found = jnp.int32(0)
        for b in starts[s]:
            found = jnp.where(b <= t, b, found)
        return found

    base = me * T

    for s in range(2):
        for r0 in range(0, T, 64):
            pos = base + r0 + iota((64, 128), 0)
            found = jnp.zeros((64, 128), jnp.int32)
            for b in starts[s]:
                found = jnp.where(pos >= b, b, found)
            lo[s, r0:r0 + 64, :] = found - base
        for h in range(2):
            vv[2 * s + h, :, HEAD:] = jnp.ones((T, HEAD), bf16)

    wbuf[320:384, :] = jnp.zeros((64, wbuf.shape[1]), bf16)

    def ready():
        for i in range(5):
            small(i).wait()
        for j in range(3):
            row = conv[j:j + 1, :]
            taps[j:j + 1, 0:128] = row[:, 32:160]
            taps[j:j + 1, 128:256] = row[:, 192:320]
            taps[j:j + 1, 256:384] = jnp.concatenate(
                [row[:, 0:32], row[:, 160:192], jnp.zeros((1, 64), f32)], axis=1)

    def project(s, c):
        fetch(s, c).wait()
        low = nt(hbuf[s, c * CHUNK:(c + 1) * CHUNK, :], wbuf[...]).astype(bf16)
        qkv[s, RIM + c * CHUNK:RIM + (c + 1) * CHUNK, :] = low.astype(f32)
        if c == C - 1:
            rim_s[s] = low[CHUNK - RIM:, :]

    rim = pltpu.make_async_remote_copy(rim_s, rim_r, rim_sem.at[0], rim_sem.at[1], device_id=nxt, device_id_type=MESH)

    def mix(s, c):
        for r0 in range(c * CHUNK, (c + 1) * CHUNK, 64):
            first = lo[s, r0:r0 + 64, :]
            pos = r0 + iota((64, 128), 0)
            one_back = first < pos
            two_back = first < pos - 1
            for j in range(3):
                lanes = slice(128 * j, 128 * j + 128)
                x0 = qkv[s, RIM + r0:RIM + r0 + 64, lanes]
                x1 = qkv[s, RIM + r0 - 1:RIM + r0 + 63, lanes]
                x2 = qkv[s, RIM + r0 - 2:RIM + r0 + 62, lanes]
                m = taps[0:1, lanes] * x0
                m = m + taps[1:2, lanes] * jnp.where(one_back, x1, 0.0)
                m = m + taps[2:3, lanes] * jnp.where(two_back, x2, 0.0)
                if j < 2:
                    vv[2 * s + j, r0:r0 + 64, 0:HEAD] = m.astype(bf16)
                else:
                    m = jnp.where(iota((64, 128), 1) == ONE, 1.0, m)
                    qk[s, r0:r0 + 64, :] = m.astype(bf16)

    def summarise(s, h):
        g = 2 * s + h
        inside = begin_of(s, base + T - 1) - base
        total = jnp.zeros((KEPT, 2 * HEAD), f32)
        for c in range(C):
            rows = slice(c * CHUNK, (c + 1) * CHUNK)
            wide = nt(ek[h], qk[s, rows, :])
            phi = wide[:KEPT] * wide[KEPT:]
            phi = jnp.where(c * CHUNK + iota((KEPT, CHUNK), 1) >= inside, phi, 0.0).astype(bf16)
            total = total + nn(phi, vv[g, rows, :])
        state, norm = total[:, :HEAD], total[:, HEAD:]
        f, l = iota((KEPT, HEAD), 0), iota((KEPT, HEAD), 1)
        n0 = jnp.sum(jnp.where(f == l, norm, 0.0), axis=0, keepdims=True)
        n1 = jnp.sum(jnp.where(f == l + HEAD, norm, 0.0), axis=0, keepdims=True)
        state = jnp.where(f == ZROW, n0, jnp.where(f == ZROW + 1, n1, state)).astype(bf16)
        lbuf[s, 2 * h] = state[:PIECE]
        lbuf[s, 2 * h + 1] = state[PIECE:]

    def p1(s, k):
        return pltpu.make_async_remote_copy(
            lbuf.at[s, lax.rem(y + k, ROW)], xbuf.at[s, k - 1], p1s.at[s, k - 1], p1r.at[s, k - 1],
            device_id=along_y(k), device_id_type=MESH)

    def p2(s, k):
        return pltpu.make_async_remote_copy(
            rsend.at[s], zbuf.at[s, k - 1], p2s.at[s, k - 1], p2r.at[s, k - 1],
            device_id=along_z(k), device_id_type=MESH)

    def p3(s, k):
        return pltpu.make_async_remote_copy(
            esend.at[s, k - 1], ebuf.at[s, y], p3s.at[s, k - 1], p3r.at[s, k - 1],
            device_id=along_y(k), device_id_type=MESH)

    def p3_in(s, k):
        return pltpu.make_async_remote_copy(
            esend.at[s, k - 1], ebuf.at[s, lax.rem(y - k + ROW, ROW)], p3s.at[s, k - 1], p3r.at[s, k - 1],
            device_id=along_y(k), device_id_type=MESH)

    def ss(s, k):
        return pltpu.make_async_remote_copy(
            ssb.at[s], ssr.at[s, k - 1], sss.at[s, k - 1], ssrs.at[s, k - 1],
            device_id=along_h(k), device_id_type=MESH)

    rowbase = z * (ROW * T)

    def last_of(j):
        return rowbase + (j + 1) * T - 1

    def gathered(s):
        parts = [lbuf[s, y].astype(f32)]
        places = [y]
        for k in (1, 2, 3):
            parts.append(xbuf[s, k - 1].astype(f32))
            places.append(lax.rem(y - k + ROW, ROW))
        return parts, places

    def row_sum(s):
        for k in (1, 2, 3):
            p1(s, k).wait_recv()
        parts, places = gathered(s)
        begin = begin_of(s, last_of(ROW - 1))
        total = jnp.zeros((PIECE, HEAD), f32)
        for part, j in zip(parts, places):
            total = total + jnp.where(begin <= last_of(j), part, 0.0)
        rsend[s] = total.astype(bf16)
        for k in (1, 2):
            p2(s, k).start()

    def entering(s):
        for k in (1, 2):
            p2(s, k).wait_recv()
        parts, places = gathered(s)
        one, two = zbuf[s, 0].astype(f32), zbuf[s, 1].astype(f32)
        for k in (1, 2, 3, 0):
            target = lax.rem(y + k, ROW)
            begin = begin_of(s, rowbase + target * T)
            total = jnp.where(begin < rowbase, one, 0.0) + jnp.where(begin < rowbase - ROW * T, two, 0.0)
            for part, j in zip(parts, places):
                reach = jnp.where(j < target, last_of(j), -1)
                total = total + jnp.where(begin <= reach, part, 0.0)
            if k:
                esend[s, k - 1] = total.astype(bf16)
                p3(s, k).start()
            else:
                ebuf[s, y] = total.astype(bf16)

    def attend(s, h):
        g = 2 * s + h
        for c in range(C):
            rows = slice(c * CHUNK, (c + 1) * CHUNK)
            q = qk[s, rows, :]
            first = jnp.concatenate([lo[s, rows, :]] * (CHUNK // 128), axis=1)
            cols = iota((CHUNK, CHUNK), 1)
            parts = []
            for b in range(c + 1):
                u = nt(q, kk[g, b * CHUNK:(b + 1) * CHUNK, :])
                u = u * u + 0.0625
                keep = cols + b * CHUNK >= first
                if b == c:
                    keep = keep & (cols <= iota((CHUNK, CHUNK), 0))
                parts.append(jnp.where(keep, u, 0.0).astype(bf16))
            weights = parts[0] if c == 0 else jnp.concatenate(parts, axis=1)
            nd[g, rows, :] = nn(weights, vv[g, :(c + 1) * CHUNK, :])

    def queries(s, h):
        g = 2 * s + h
        for c in range(C):
            rows = slice(c * CHUNK, (c + 1) * CHUNK)
            ab = nn(qk[s, rows, :], eq[h])
            phq[g, rows, :] = (ab[:, :256] * ab[:, 256:]).astype(bf16)

    def keys(s, h):
        for c in range(C):
            rows = slice(c * CHUNK, (c + 1) * CHUNK)
            kk[2 * s + h, rows, :] = nn(qk[s, rows, :], mk[h]).astype(bf16)

    def finish(s):
        for k in (1, 2, 3):
            p3_in(s, k).wait_recv()
        rhs = []
        f, l = iota((KEPT, HEAD), 0), iota((KEPT, HEAD), 1)
        for h in range(2):
            state = jnp.concatenate([ebuf[s, 2 * h], ebuf[s, 2 * h + 1]], axis=0)
            wide = state.astype(f32)
            n0, n1 = wide[ZROW:ZROW + 1], wide[ZROW + 1:ZROW + 2]
            norm = jnp.sum(jnp.where(f == l, n0, 0.0) + jnp.where(f == l + HEAD, n1, 0.0), axis=1, keepdims=True)
            norm = jnp.broadcast_to(norm, (KEPT, HEAD)).astype(bf16)
            both = jnp.concatenate([state, norm], axis=1)
            rhs.append(jnp.concatenate([both, jnp.zeros((256 - KEPT, 256), bf16)], axis=0))
        eye = iota((128, 128), 0) == iota((128, 128), 1)
        for r0 in range(0, T, 128):
            rows = slice(r0, r0 + 128)
            use = lo[s, rows, :] < 0
            squares = jnp.zeros((128, 128), f32)
            for h in range(2):
                g = 2 * s + h
                came = nn(phq[g, rows, :], rhs[h])
                num = nd[g, rows, :HEAD] + jnp.where(use, came[:, :HEAD], 0.0)
                den = nd[g, rows, HEAD:] + jnp.where(use, came[:, HEAD:], 0.0)
                a = num / den
                att[s, rows, h * HEAD:(h + 1) * HEAD] = a
                squares = squares + a * a
            col = jnp.sum(squares, axis=1, keepdims=True)
            i = r0 // 128
            ssb[s, i:i + 1, :] = jnp.sum(jnp.where(eye, col, 0.0), axis=0, keepdims=True)
        for k in range(1, hn):
            ss(s, k).start()

    def write(s, c):
        rows = pl.ds(c * CHUNK, CHUNK)
        return pltpu.make_async_copy(obuf.at[s, rows], out.at[s, rows], osem.at[s, c])

    def scale(s):
        for k in range(1, hn):
            ss(s, k).wait_recv()
        total = ssb[s]
        for k in range(1, hn):
            total = total + ssr[s, k - 1]
        factor = lax.rsqrt(total / (hn * 2 * HEAD) + 1e-06)
        eye = iota((128, 128), 0) == iota((128, 128), 1)
        g = gain[...].astype(f32).reshape(1, 2 * HEAD)
        for r0 in range(0, T, 128):
            i = r0 // 128
            rows = slice(r0, r0 + 128)
            col = jnp.sum(jnp.where(eye, factor[i:i + 1, :], 0.0), axis=1, keepdims=True)
            obuf[s, rows, :] = (att[s, rows, :] * col * g).astype(bf16)
            if (r0 + 128) % CHUNK == 0:
                write(s, r0 // CHUNK).start()

    def columns_in():
        for i in range(4):
            columns(i).wait()

    def greet():
        pl.semaphore_wait(barrier, len(sources))

    def rim_in():
        rim.wait_recv()
        for s in range(2):
            qkv[s, 0:RIM, :] = rim_r[s].astype(f32)

    def pieces_out(s):
        for k in (1, 2, 3):
            p1(s, k).start()

    def drain():
        for s in range(2):
            for c in range(C):
                write(s, c).wait()
        rim.wait_send()
        for s in range(2):
            for k in (1, 2, 3):
                p1(s, k).wait_send()
                p3(s, k).wait_send()
            for k in (1, 2):
                p2(s, k).wait_send()
            for k in range(1, hn):
                ss(s, k).wait_send()

    plan = [(columns_in,), (project, 0, C - 1), (project, 1, C - 1), (greet,), (rim.start,), (ready,)]
    plan += [(project, 0, c) for c in range(C - 1)]
    plan += [(mix, 0, c) for c in range(1, C)]
    plan += [(rim_in,), (mix, 0, 0), (summarise, 0, 0), (summarise, 0, 1), (pieces_out, 0)]
    plan += [(project, 1, c) for c in range(C - 1)]
    plan += [(mix, 1, c) for c in range(C)]
    plan += [(summarise, 1, 0), (summarise, 1, 1), (pieces_out, 1)]
    plan += [(row_sum, 0), (keys, 0, 0), (attend, 0, 0), (row_sum, 1), (keys, 0, 1), (attend, 0, 1)]
    plan += [(entering, 0), (queries, 0, 0), (queries, 0, 1), (keys, 1, 0), (attend, 1, 0)]
    plan += [(entering, 1), (queries, 1, 0), (queries, 1, 1), (keys, 1, 1), (attend, 1, 1)]
    plan += [(finish, 0), (finish, 1), (scale, 0), (scale, 1), (drain,)]
    for step, *where in plan:
        step(*where)


def shards(zn, hn, hidden, w_qkv, conv_weight, norm_gain, repo_lengths):
    seqs, T, D = hidden.shape
    C = T // CHUNK
    query, key, move = tables()
    any_spec = pl.BlockSpec(memory_space=pl.ANY)
    dma = pltpu.SemaphoreType.DMA
    return pl.pallas_call(
        functools.partial(kernel, zn, hn),
        out_shape=jax.ShapeDtypeStruct((seqs, T, 2 * HEAD), bf16),
        in_specs=[any_spec] * 4 + [pl.BlockSpec(memory_space=pltpu.SMEM)] + [any_spec] * 3,
        out_specs=any_spec,
        scratch_shapes=[
            pltpu.VMEM((2, T, D), bf16),
            pltpu.VMEM((384, D), bf16),
            pltpu.VMEM(conv_weight.shape, f32),
            pltpu.VMEM(norm_gain.shape, bf16),
            pltpu.VMEM(query.shape, bf16),
            pltpu.VMEM(key.shape, bf16),
            pltpu.VMEM(move.shape, bf16),
            pltpu.VMEM((8, 384), f32),
            pltpu.VMEM((2, RIM + T, 384), f32),
            pltpu.VMEM((2, T, 128), jnp.int32),
            pltpu.VMEM((2, T, 128), bf16),
            pltpu.VMEM((4, T, 128), bf16),
            pltpu.VMEM((4, T, 256), bf16),
            pltpu.VMEM((4, T, 256), bf16),
            pltpu.VMEM((4, T, 256), f32),
            pltpu.VMEM((2, T, 256), f32),
            pltpu.VMEM((2, RIM, 384), bf16),
            pltpu.VMEM((2, RIM, 384), bf16),
            pltpu.VMEM((2, ROW, PIECE, HEAD), bf16),
            pltpu.VMEM((2, 3, PIECE, HEAD), bf16),
            pltpu.VMEM((2, PIECE, HEAD), bf16),
            pltpu.VMEM((2, 2, PIECE, HEAD), bf16),
            pltpu.VMEM((2, 3, PIECE, HEAD), bf16),
            pltpu.VMEM((2, ROW, PIECE, HEAD), bf16),
            pltpu.VMEM((2, T // 128, 128), f32),
            pltpu.VMEM((2, max(hn - 1, 1), T // 128, 128), f32),
            pltpu.VMEM((2, T, 256), bf16),
            dma((4,)),
            dma((5,)),
            dma((2, C)),
            dma((2, C)),
            dma((2,)),
            dma((2, 3)),
            dma((2, 3)),
            dma((2, 2)),
            dma((2, 2)),
            dma((2, 3)),
            dma((2, 3)),
            dma((2, max(hn - 1, 1))),
            dma((2, max(hn - 1, 1))),
        ],
        compiler_params=pltpu.CompilerParams(
            collective_id=0, has_side_effects=True, vmem_limit_bytes=60 * 1024 * 1024),
        name="packed_linear_attention",
    )(hidden, w_qkv.T, conv_weight, norm_gain, repo_lengths,
      jnp.asarray(query), jnp.asarray(key), jnp.asarray(move))


def solution(mesh):
    zn, hn = mesh.shape["seq"] // ROW, mesh.shape["head"]
    in_specs = (P(None, "seq", None), P(None, "head"), P(None, "head"), P("head"), P())
    out_specs = P(None, "seq", "head")
    return jax.shard_map(
        functools.partial(shards, zn, hn), mesh=mesh, in_specs=in_specs, out_specs=out_specs, check_vma=False)
```

```python
import functools
import jax
import jax.numpy as jnp
import numpy as np
from jax import lax
from jax.experimental import pallas as pl
from jax.experimental.pallas import tpu as pltpu
from jax.sharding import PartitionSpec as P

FEAT = 16
HEAD = 128
WIDTH = 2 * FEAT + HEAD
NSEG = 12
ROW = 4
CHUNK = 256
RIM = 16
KEPT = 160
PIECE = 80
ONE = 64
QUAD = 136
ZROW = 137
LINEAR = 144
MESH = pl.DeviceIdType.MESH
bf16 = jnp.bfloat16
f32 = jnp.float32


def tables():
    query = np.zeros((2, 128, 512), np.float32)
    move = np.zeros((2, 128, 128), np.float32)
    for h in range(2):
        qb, kb = 32 * h, 32 * h + FEAT
        for f in range(QUAD):
            d, i = f // FEAT, f % FEAT
            query[h, qb + i, f] = 1 / 8 if d else 1 / 16
            query[h, qb + (i + d) % FEAT, 256 + f] = 1.0
        query[h, ONE, QUAD] = 1.0
        query[h, ONE, 256 + QUAD] = 1.0
        for i in range(FEAT):
            query[h, qb + i, LINEAR + i] = 1 / 4
            query[h, ONE, 256 + LINEAR + i] = 1.0
            move[h, qb + i, kb + i] = 1 / 16
        move[h, ONE, ONE] = 1 / 4
    return query.astype(jnp.bfloat16), move.astype(jnp.bfloat16)


def nt(a, b):
    return lax.dot_general(a, b, (((1,), (1,)), ((), ())), preferred_element_type=f32)


def nn(a, b):
    return jnp.dot(a, b, preferred_element_type=f32)


def iota(shape, dim):
    return lax.broadcasted_iota(jnp.int32, shape, dim)


def kernel(zn, hn, hid, wq, conv_in, lengths_in, eq_in, mk_in, att, fac,
           hbuf, wbuf, conv, lengths, eq, mk, taps, kd, qkv, lor, loc, qkt, qk, kk, vv, phq, nd, rim_s, rim_r, lbuf, xbuf,
           rsend, zbuf, esend, ebuf, ssb, ssr,
           wsem, csem, hsem, rim_sem, p1s, p1r, p2s, p2r, p3s, p3r, sss, ssrs):
    T = hbuf.shape[1]
    C = T // CHUNK
    G = T // 128
    me = lax.axis_index("seq")
    hd = lax.axis_index("head")
    z = me // ROW
    y = lax.rem(me, ROW)

    def at_seq(i):
        return (i, hd)

    def along_y(k):
        return (z * ROW + lax.rem(y + k + ROW, ROW), hd)

    def along_z(k):
        return (lax.rem(z + k + zn, zn) * ROW + y, hd)

    def along_h(k):
        return (me, lax.rem(hd + k + hn, hn))

    nxt = at_seq(lax.rem(me + 1, zn * ROW))
    prv = at_seq(lax.rem(me + zn * ROW - 1, zn * ROW))

    wcopy = pltpu.make_async_copy(wq, wbuf, wsem)

    def small(i):
        source, target = ((lengths_in, lengths), (conv_in, conv), (mk_in, mk), (eq_in, eq))[i]
        return pltpu.make_async_copy(source, target, csem.at[i])

    small(0).start()
    small(1).start()
    wcopy.start()
    order = [(0, C - 1), (1, C - 1)] + [(0, c) for c in range(C - 1)] + [(1, c) for c in range(C - 1)]

    def fetch(s, c):
        rows = pl.ds(c * CHUNK, CHUNK)
        return pltpu.make_async_copy(hid.at[s, rows], hbuf.at[s, rows], hsem.at[s, c])

    for n, (s, c) in enumerate(order):
        fetch(s, c).start()
        if n == 1:
            for i in range(2, 4):
                small(i).start()

    barrier = pltpu.get_barrier_semaphore()
    sources = [prv] + [along_y(-k) for k in (1, 2, 3)] + [along_z(-k) for k in (1, 2)]
    sources += [along_h(-k) for k in range(1, hn)]
    for d in sources:
        pl.semaphore_signal(barrier, inc=1, device_id=d, device_id_type=MESH)

    starts = []

    def bounds():
        small(0).wait()
        for s in range(2):
            run = jnp.int32(0)
            own = []
            for r in range(NSEG - 1):
                run = run + lengths[s, r]
                own.append(run)
            starts.append(own)

    def begin_of(s, t):
        found = jnp.int32(0)
        for b in starts[s]:
            found = jnp.where(b <= t, b, found)
        return found

    base = me * T

    def places(s, pos):
        found = jnp.zeros(pos.shape, jnp.int32)
        for b in starts[s]:
            found = jnp.where(pos >= b, b, found)
        return found - base

    def prepare():
        for s in range(2):
            lor[s] = places(s, base + iota((8, T), 1))
            qkt[s, ONE:ONE + 16, :] = jnp.where(iota((16, T), 0) == 0, 1.0, 0.0).astype(bf16)
            qkt[s, ONE + 16:, :] = jnp.zeros((128 - ONE - 16, T), bf16)
            for h in range(2):
                vv[2 * s + h, HEAD:, :] = jnp.ones((HEAD, T), bf16)
        small(1).wait()
        for j in range(3):
            for c0 in range(0, 2 * WIDTH, 64):
                row = jnp.broadcast_to(conv[j:j + 1, c0:c0 + 64], (64, 64))
                eye = iota((64, 64), 0) == iota((64, 64), 1)
                col = jnp.sum(jnp.where(eye, row, 0.0), axis=1, keepdims=True)
                taps[j, c0:c0 + 64, :] = jnp.broadcast_to(col, (64, 128))

    def ready():
        for i in range(2, 4):
            small(i).wait()

    def columns_in():
        wcopy.wait()

    def arrive(s, c):
        fetch(s, c).wait()

    def project(s, low_c, high_c):
        rows = slice(low_c * CHUNK, high_c * CHUNK)
        low = nt(wbuf[...], hbuf[s, rows, :]).astype(bf16)
        qkv[s, :, 128 + low_c * CHUNK:128 + high_c * CHUNK] = low.astype(f32)
        if high_c == C:
            pick = jnp.where(iota((RIM, 128), 1) == iota((RIM, 128), 0) + 128 - RIM, 1.0, 0.0).astype(bf16)
            rim_s[s] = nt(pick, low[:, low.shape[1] - 128:]).astype(bf16)

    rim = pltpu.make_async_remote_copy(rim_s, rim_r, rim_sem.at[0], rim_sem.at[1], device_id=nxt, device_id_type=MESH)

    def rim_in():
        rim.wait_recv()
        pick = jnp.where(iota((RIM, 128), 1) == iota((RIM, 128), 0) + 128 - RIM, 1.0, 0.0).astype(bf16)
        for s in range(2):
            qkv[s, :, 0:128] = lax.dot_general(
                rim_r[s], pick, (((0,), (0,)), ((), ())), preferred_element_type=f32)

    def mix(s, c):
        lanes = slice(c * CHUNK, (c + 1) * CHUNK)
        first = jnp.concatenate([lor[s, :, lanes]] * 4, axis=0)
        pos = c * CHUNK + iota((32, CHUNK), 1)
        one_back = first < pos
        two_back = first < pos - 1
        for r0 in range(0, 2 * WIDTH, 32):
            rows = slice(r0, r0 + 32)
            ext = qkv[s, rows, c * CHUNK:(c + 1) * CHUNK + 128]
            x1 = pltpu.roll(ext, 1, 1)[:, 128:]
            x2 = pltpu.roll(ext, 2, 1)[:, 128:]

            def tap(j):
                return jnp.concatenate([taps[j, rows, :]] * (CHUNK // 128), axis=1)

            m = tap(0) * ext[:, 128:]
            m = m + tap(1) * jnp.where(one_back, x1, 0.0)
            m = m + tap(2) * jnp.where(two_back, x2, 0.0)
            m = m.astype(bf16)
            h, d = r0 // WIDTH, r0 % WIDTH
            if d == 0:
                qkt[s, 32 * h:32 * h + 32, lanes] = m
            else:
                vv[2 * s + h, d - 32:d, lanes] = m

    def summarise(s):
        inside = begin_of(s, base + T - 1) - base
        for h in range(2):
            g = 2 * s + h
            key = qkt[s, 32 * h + FEAT:32 * h + 2 * FEAT, :].astype(f32)
            key = jnp.where(iota((FEAT, T), 1) >= inside, key, 0.0)
            small_key = key * (1.0 / 16.0)
            kd[g, 0:FEAT, :] = small_key
            kd[g, FEAT:2 * FEAT, :] = small_key
            blocks = [(key * kd[g, d:d + FEAT, :]).astype(bf16) for d in range(8)]
            here = (iota((8, T), 1) >= inside) & (iota((8, T), 0) == 0)
            last = [key[:8] * kd[g, 8:16, :], jnp.where(here, 0.125, 0.0)]
            blocks.append(jnp.concatenate(last, axis=0).astype(bf16))
            blocks.append((key * 0.125).astype(bf16))
            total = nt(jnp.concatenate(blocks, axis=0), vv[g])
            state, norm = total[:, :HEAD], total[:, HEAD:]
            f, l = iota((KEPT, HEAD), 0), iota((KEPT, HEAD), 1)
            n0 = jnp.sum(jnp.where(f == l, norm, 0.0), axis=0, keepdims=True)
            n1 = jnp.sum(jnp.where(f == l + HEAD, norm, 0.0), axis=0, keepdims=True)
            state = jnp.where(f == ZROW, n0, jnp.where(f == ZROW + 1, n1, state)).astype(bf16)
            lbuf[s, 2 * h] = state[:PIECE]
            lbuf[s, 2 * h + 1] = state[PIECE:]

    def p1(s, k):
        return pltpu.make_async_remote_copy(
            lbuf.at[s, lax.rem(y + k, ROW)], xbuf.at[s, k - 1], p1s.at[s, k - 1], p1r.at[s, k - 1],
            device_id=along_y(k), device_id_type=MESH)

    def p2(s, k):
        return pltpu.make_async_remote_copy(
            rsend.at[s], zbuf.at[s, k - 1], p2s.at[s, k - 1], p2r.at[s, k - 1],
            device_id=along_z(k), device_id_type=MESH)

    def p3(s, k):
        return pltpu.make_async_remote_copy(
            esend.at[s, k - 1], ebuf.at[s, y], p3s.at[s, k - 1], p3r.at[s, k - 1],
            device_id=along_y(k), device_id_type=MESH)

    def p3_in(s, k):
        return pltpu.make_async_remote_copy(
            esend.at[s, k - 1], ebuf.at[s, lax.rem(y - k + ROW, ROW)], p3s.at[s, k - 1], p3r.at[s, k - 1],
            device_id=along_y(k), device_id_type=MESH)

    def ss(s, k):
        return pltpu.make_async_remote_copy(
            ssb.at[s], ssr.at[s, k - 1], sss.at[s, k - 1], ssrs.at[s, k - 1],
            device_id=along_h(k), device_id_type=MESH)

    rowbase = z * (ROW * T)

    def last_of(j):
        return rowbase + (j + 1) * T - 1

    def gathered(s):
        parts = [lbuf[s, y].astype(f32)]
        owners = [y]
        for k in (1, 2, 3):
            parts.append(xbuf[s, k - 1].astype(f32))
            owners.append(lax.rem(y - k + ROW, ROW))
        return parts, owners

    def row_sum(s):
        for k in (1, 2, 3):
            p1(s, k).wait_recv()
        parts, owners = gathered(s)
        begin = begin_of(s, last_of(ROW - 1))
        total = jnp.zeros((PIECE, HEAD), f32)
        for part, j in zip(parts, owners):
            total = total + jnp.where(begin <= last_of(j), part, 0.0)
        rsend[s] = total.astype(bf16)
        for k in (1, 2):
            p2(s, k).start()

    def entering(s):
        for k in (1, 2):
            p2(s, k).wait_recv()
        parts, owners = gathered(s)
        one, two = zbuf[s, 0].astype(f32), zbuf[s, 1].astype(f32)
        for k in (1, 2, 3, 0):
            target = lax.rem(y + k, ROW)
            begin = begin_of(s, rowbase + target * T)
            total = jnp.where(begin < rowbase, one, 0.0) + jnp.where(begin < rowbase - ROW * T, two, 0.0)
            for part, j in zip(parts, owners):
                reach = jnp.where(j < target, last_of(j), -1)
                total = total + jnp.where(begin <= reach, part, 0.0)
            if k:
                esend[s, k - 1] = total.astype(bf16)
                p3(s, k).start()
            else:
                ebuf[s, y] = total.astype(bf16)

    def attend(s, h):
        g = 2 * s + h
        for c in range(C):
            rows = slice(c * CHUNK, (c + 1) * CHUNK)
            q = qk[s, rows, :]
            first = jnp.concatenate([loc[s, rows, :]] * (CHUNK // 128), axis=1)
            cols = iota((CHUNK, CHUNK), 1)
            parts = []
            for b in range(c + 1):
                u = nn(q, kk[g, :, b * CHUNK:(b + 1) * CHUNK])
                u = u * u + 0.0625
                keep = cols + b * CHUNK >= first
                if b == c:
                    keep = keep & (cols <= iota((CHUNK, CHUNK), 0))
                parts.append(jnp.where(keep, u, 0.0).astype(bf16))
            weights = parts[0] if c == 0 else jnp.concatenate(parts, axis=1)
            nd[g, rows, :] = nt(weights, vv[g, :, :(c + 1) * CHUNK])

    def queries(s, h):
        g = 2 * s + h
        for c in range(C):
            rows = slice(c * CHUNK, (c + 1) * CHUNK)
            ab = nn(qk[s, rows, :], eq[h])
            phq[g, rows, :] = (ab[:, :256] * ab[:, 256:]).astype(bf16)

    def turn(s):
        for r0 in range(0, T, 64):
            loc[s, r0:r0 + 64, :] = places(s, base + r0 + iota((64, 128), 0))
        same = jnp.where(iota((CHUNK, CHUNK), 0) == iota((CHUNK, CHUNK), 1), 1.0, 0.0).astype(bf16)
        for c in range(C):
            rows = slice(c * CHUNK, (c + 1) * CHUNK)
            qk[s, rows, :] = nt(same, qkt[s, :, rows]).astype(bf16)
        for h in range(2):
            kk[2 * s + h] = nn(mk[h], qkt[s]).astype(bf16)

    def finish(s):
        for k in (1, 2, 3):
            p3_in(s, k).wait_recv()
        rhs = []
        f, l = iota((KEPT, HEAD), 0), iota((KEPT, HEAD), 1)
        for h in range(2):
            state = jnp.concatenate([ebuf[s, 2 * h], ebuf[s, 2 * h + 1]], axis=0)
            wide = state.astype(f32)
            n0, n1 = wide[ZROW:ZROW + 1], wide[ZROW + 1:ZROW + 2]
            norm = jnp.sum(jnp.where(f == l, n0, 0.0) + jnp.where(f == l + HEAD, n1, 0.0), axis=1, keepdims=True)
            norm = jnp.broadcast_to(norm, (KEPT, HEAD)).astype(bf16)
            both = jnp.concatenate([state, norm], axis=1)
            rhs.append(jnp.concatenate([both, jnp.zeros((256 - KEPT, 256), bf16)], axis=0))
        eye = iota((128, 128), 0) == iota((128, 128), 1)
        for r0 in range(0, T, 128):
            rows = slice(r0, r0 + 128)
            use = loc[s, rows, :] < 0
            squares = jnp.zeros((128, 128), f32)
            for h in range(2):
                g = 2 * s + h
                came = nn(phq[g, rows, :], rhs[h])
                num = nd[g, rows, :HEAD] + jnp.where(use, came[:, :HEAD], 0.0)
                den = nd[g, rows, HEAD:] + jnp.where(use, came[:, HEAD:], 0.0)
                a = num / den
                att[s, rows, h * HEAD:(h + 1) * HEAD] = a
                squares = squares + a * a
            col = jnp.sum(squares, axis=1, keepdims=True)
            i = r0 // 128
            ssb[s, i:i + 1, :] = jnp.sum(jnp.where(eye, col, 0.0), axis=0, keepdims=True)
        for k in range(1, hn):
            ss(s, k).start()

    def scale(s):
        for k in range(1, hn):
            ss(s, k).wait_recv()
        total = ssb[s]
        for k in range(1, hn):
            total = total + ssr[s, k - 1]
        fac[s] = lax.rsqrt(total / (hn * 2 * HEAD) + 1e-06)

    def greet():
        pl.semaphore_wait(barrier, len(sources))

    def pieces_out(s):
        for k in (1, 2, 3):
            p1(s, k).start()

    def drain():
        rim.wait_send()
        for s in range(2):
            for k in (1, 2, 3):
                p1(s, k).wait_send()
                p3(s, k).wait_send()
            for k in (1, 2):
                p2(s, k).wait_send()
            for k in range(1, hn):
                ss(s, k).wait_send()

    plan = [(bounds,), (prepare,), (columns_in,), (arrive, 0, C - 1), (arrive, 1, C - 1)]
    plan += [(project, 0, C - 1, C), (project, 1, C - 1, C), (greet,), (rim.start,)]
    plan += [(arrive, 0, c) for c in range(C - 1)] + [(project, 0, 0, C - 1)]
    plan += [(arrive, 1, c) for c in range(C - 1)] + [(project, 1, 0, C - 1)]
    plan += [(mix, 0, c) for c in range(1, C)] + [(mix, 1, c) for c in range(1, C)]
    plan += [(rim_in,), (mix, 0, 0), (mix, 1, 0), (summarise, 0), (pieces_out, 0), (summarise, 1), (pieces_out, 1)]
    plan += [(ready,), (turn, 0), (turn, 1), (attend, 0, 0)]
    plan += [(row_sum, 0), (row_sum, 1), (attend, 0, 1), (attend, 1, 0)]
    plan += [(entering, 0), (entering, 1), (queries, 0, 0), (queries, 0, 1), (queries, 1, 0), (queries, 1, 1)]
    plan += [(attend, 1, 1), (finish, 0), (finish, 1), (scale, 0), (scale, 1), (drain,)]
    for step, *where in plan:
        step(*where)


def rescale(att, fac, gain, out, obuf, osem):
    T = att.shape[1]
    eye = iota((128, 128), 0) == iota((128, 128), 1)
    g = gain[...].astype(f32).reshape(1, 2 * HEAD)

    def write(s, c):
        rows = pl.ds(c * CHUNK, CHUNK)
        return pltpu.make_async_copy(obuf.at[s, rows], out.at[s, rows], osem.at[s, c])

    for s in range(2):
        for r0 in range(0, T, 128):
            i = r0 // 128
            rows = slice(r0, r0 + 128)
            col = jnp.sum(jnp.where(eye, fac[s, i:i + 1, :], 0.0), axis=1, keepdims=True)
            obuf[s, rows, :] = (att[s, rows, :] * col * g).astype(bf16)
            if (r0 + 128) % CHUNK == 0:
                write(s, r0 // CHUNK).start()
    for s in range(2):
        for c in range(T // CHUNK):
            write(s, c).wait()


def shards(zn, hn, hidden, w_qkv, conv_weight, norm_gain, repo_lengths):
    seqs, T, D = hidden.shape
    C = T // CHUNK
    query, move = tables()
    any_spec = pl.BlockSpec(memory_space=pl.ANY)
    vmem = pl.BlockSpec(memory_space=pltpu.VMEM)
    dma = pltpu.SemaphoreType.DMA

    def pin(x):
        return pltpu.with_memory_space_constraint(jnp.asarray(x), pltpu.HBM)

    att, fac = pl.pallas_call(
        functools.partial(kernel, zn, hn),
        out_shape=(jax.ShapeDtypeStruct((seqs, T, 2 * HEAD), f32), jax.ShapeDtypeStruct((seqs, T // 128, 128), f32)),
        in_specs=[any_spec] * 6,
        out_specs=(vmem, vmem),
        scratch_shapes=[
            pltpu.VMEM((2, T, D), bf16),
            pltpu.VMEM((2 * WIDTH, D), bf16),
            pltpu.VMEM(conv_weight.shape, f32),
            pltpu.SMEM(repo_lengths.shape, jnp.int32),
            pltpu.VMEM(query.shape, bf16),
            pltpu.VMEM(move.shape, bf16),
            pltpu.VMEM((3, 2 * WIDTH, 128), f32),
            pltpu.VMEM((4, 2 * FEAT, T), f32),
            pltpu.VMEM((2, 2 * WIDTH, 128 + T), f32),
            pltpu.VMEM((2, 8, T), jnp.int32),
            pltpu.VMEM((2, T, 128), jnp.int32),
            pltpu.VMEM((2, 128, T), bf16),
            pltpu.VMEM((2, T, 128), bf16),
            pltpu.VMEM((4, 128, T), bf16),
            pltpu.VMEM((4, 256, T), bf16),
            pltpu.VMEM((4, T, 256), bf16),
            pltpu.VMEM((4, T, 256), f32),
            pltpu.VMEM((2, RIM, 2 * WIDTH), bf16),
            pltpu.VMEM((2, RIM, 2 * WIDTH), bf16),
            pltpu.VMEM((2, ROW, PIECE, HEAD), bf16),
            pltpu.VMEM((2, 3, PIECE, HEAD), bf16),
            pltpu.VMEM((2, PIECE, HEAD), bf16),
            pltpu.VMEM((2, 2, PIECE, HEAD), bf16),
            pltpu.VMEM((2, 3, PIECE, HEAD), bf16),
            pltpu.VMEM((2, ROW, PIECE, HEAD), bf16),
            pltpu.VMEM((2, T // 128, 128), f32),
            pltpu.VMEM((2, max(hn - 1, 1), T // 128, 128), f32),
            dma,
            dma((4,)),
            dma((2, C)),
            dma((2,)),
            dma((2, 3)),
            dma((2, 3)),
            dma((2, 2)),
            dma((2, 2)),
            dma((2, 3)),
            dma((2, 3)),
            dma((2, max(hn - 1, 1))),
            dma((2, max(hn - 1, 1))),
        ],
        compiler_params=pltpu.CompilerParams(
            collective_id=0, has_side_effects=True, vmem_limit_bytes=44 * 1024 * 1024),
        name="packed_linear_attention",
    )(pin(hidden), pin(w_qkv.T), pin(conv_weight), pin(repo_lengths), pin(query), pin(move))
    return pl.pallas_call(
        rescale,
        out_shape=jax.ShapeDtypeStruct((seqs, T, 2 * HEAD), bf16),
        in_specs=[vmem, vmem, vmem],
        out_specs=any_spec,
        scratch_shapes=[pltpu.VMEM((2, T, 2 * HEAD), bf16), dma((2, C))],
        compiler_params=pltpu.CompilerParams(vmem_limit_bytes=8 * 1024 * 1024),
        name="rescale_rows",
    )(att, fac, norm_gain)


def solution(mesh):
    zn, hn = mesh.shape["seq"] // ROW, mesh.shape["head"]
    in_specs = (P(None, "seq", None), P(None, "head"), P(None, "head"), P("head"), P())
    out_specs = P(None, "seq", "head")
    return jax.shard_map(
        functools.partial(shards, zn, hn), mesh=mesh, in_specs=in_specs, out_specs=out_specs, check_vma=False)
```

```python
import functools
import jax
import jax.numpy as jnp
import numpy as np
from jax import lax
from jax.experimental import pallas as pl
from jax.experimental.pallas import tpu as pltpu
from jax.sharding import PartitionSpec as P

FEAT = 16
HEAD = 128
WIDTH = 2 * FEAT + HEAD
NSEG = 12
ROW = 4
CHUNK = 256
RIM = 16
KEPT = 160
PIECE = 80
ONE = 64
QUAD = 136
ZROW = 137
LINEAR = 144
MESH = pl.DeviceIdType.MESH
bf16 = jnp.bfloat16
f32 = jnp.float32


def tables():
    query = np.zeros((2, 128, 512), np.float32)
    move = np.zeros((2, 128, 128), np.float32)
    for h in range(2):
        qb, kb = 32 * h, 32 * h + FEAT
        for f in range(QUAD):
            d, i = f // FEAT, f % FEAT
            query[h, qb + i, f] = 1 / 8 if d else 1 / 16
            query[h, qb + (i + d) % FEAT, 256 + f] = 1.0
        query[h, ONE, QUAD] = 1.0
        query[h, ONE, 256 + QUAD] = 1.0
        for i in range(FEAT):
            query[h, qb + i, LINEAR + i] = 1 / 4
            query[h, ONE, 256 + LINEAR + i] = 1.0
            move[h, qb + i, kb + i] = 1 / 16
        move[h, ONE, ONE] = 1 / 4
    return query.astype(jnp.bfloat16), move.astype(jnp.bfloat16)


def nt(a, b):
    return lax.dot_general(a, b, (((1,), (1,)), ((), ())), preferred_element_type=f32)


def nn(a, b):
    return jnp.dot(a, b, preferred_element_type=f32)


def iota(shape, dim):
    return lax.broadcasted_iota(jnp.int32, shape, dim)


def kernel(zn, hn, hid, wq, conv_in, lengths_in, eq_in, mk_in, att, fac,
           hbuf, wbuf, conv, lengths, eq, mk, taps, kd, partial, qkv, lor, loc, qkt, qk, kk, vv, phq, nd, rim_s, rim_r, lbuf, xbuf,
           rsend, zbuf, esend, ebuf, ssb, ssr,
           wsem, csem, hsem, rim_sem, p1s, p1r, p2s, p2r, p3s, p3r, sss, ssrs):
    T = hbuf.shape[1]
    C = T // CHUNK
    G = T // 128
    me = lax.axis_index("seq")
    hd = lax.axis_index("head")
    z = me // ROW
    y = lax.rem(me, ROW)

    def at_seq(i):
        return (i, hd)

    def along_y(k):
        return (z * ROW + lax.rem(y + k + ROW, ROW), hd)

    def along_z(k):
        return (lax.rem(z + k + zn, zn) * ROW + y, hd)

    def along_h(k):
        return (me, lax.rem(hd + k + hn, hn))

    nxt = at_seq(lax.rem(me + 1, zn * ROW))
    prv = at_seq(lax.rem(me + zn * ROW - 1, zn * ROW))

    wcopy = pltpu.make_async_copy(wq, wbuf, wsem)

    def small(i):
        source, target = ((lengths_in, lengths), (conv_in, conv), (mk_in, mk), (eq_in, eq))[i]
        return pltpu.make_async_copy(source, target, csem.at[i])

    small(0).start()
    small(1).start()
    wcopy.start()
    def fetch(s, c):
        rows = pl.ds(c * CHUNK, CHUNK)
        return pltpu.make_async_copy(hid.at[s, rows], hbuf.at[s, rows], hsem.at[s, c])

    def request(s, c):
        fetch(s, c).start()

    request(0, C - 1)
    request(1, C - 1)

    barrier = pltpu.get_barrier_semaphore()
    sources = [prv] + [along_y(-k) for k in (1, 2, 3)] + [along_z(-k) for k in (1, 2)]
    sources += [along_h(-k) for k in range(1, hn)]
    for d in sources:
        pl.semaphore_signal(barrier, inc=1, device_id=d, device_id_type=MESH)

    starts = []

    def bounds():
        small(0).wait()
        for s in range(2):
            run = jnp.int32(0)
            own = []
            for r in range(NSEG - 1):
                run = run + lengths[s, r]
                own.append(run)
            starts.append(own)

    def begin_of(s, t):
        found = jnp.int32(0)
        for b in starts[s]:
            found = jnp.where(b <= t, b, found)
        return found

    base = me * T

    def places(s, pos):
        found = jnp.zeros(pos.shape, jnp.int32)
        for b in starts[s]:
            found = jnp.where(pos >= b, b, found)
        return found - base

    def prepare():
        for s in range(2):
            lor[s] = places(s, base + iota((8, T), 1))
            qkt[s, ONE:ONE + 16, :] = jnp.where(iota((16, T), 0) == 0, 1.0, 0.0).astype(bf16)
            qkt[s, ONE + 16:, :] = jnp.zeros((128 - ONE - 16, T), bf16)
            for h in range(2):
                vv[2 * s + h, HEAD:, :] = jnp.ones((HEAD, T), bf16)
        small(1).wait()
        for j in range(3):
            for c0 in range(0, 2 * WIDTH, 64):
                row = jnp.broadcast_to(conv[j:j + 1, c0:c0 + 64], (64, 64))
                eye = iota((64, 64), 0) == iota((64, 64), 1)
                col = jnp.sum(jnp.where(eye, row, 0.0), axis=1, keepdims=True)
                taps[j, c0:c0 + 64, :] = jnp.broadcast_to(col, (64, 128))

    def ready():
        for i in range(2, 4):
            small(i).wait()

    def tables_in():
        for i in range(2, 4):
            small(i).start()

    def columns_in():
        wcopy.wait()

    def arrive(s, c):
        fetch(s, c).wait()

    def project(s, low_c, high_c):
        rows = slice(low_c * CHUNK, high_c * CHUNK)
        low = nt(wbuf[...], hbuf[s, rows, :]).astype(bf16)
        qkv[s, :, 128 + low_c * CHUNK:128 + high_c * CHUNK] = low.astype(f32)
        if high_c == C:
            pick = jnp.where(iota((RIM, 128), 1) == iota((RIM, 128), 0) + 128 - RIM, 1.0, 0.0).astype(bf16)
            rim_s[s] = nt(pick, low[:, low.shape[1] - 128:]).astype(bf16)

    rim = pltpu.make_async_remote_copy(rim_s, rim_r, rim_sem.at[0], rim_sem.at[1], device_id=nxt, device_id_type=MESH)

    def rim_in():
        rim.wait_recv()
        pick = jnp.where(iota((RIM, 128), 1) == iota((RIM, 128), 0) + 128 - RIM, 1.0, 0.0).astype(bf16)
        for s in range(2):
            qkv[s, :, 0:128] = lax.dot_general(
                rim_r[s], pick, (((0,), (0,)), ((), ())), preferred_element_type=f32)

    def mix(s, c):
        lanes = slice(c * CHUNK, (c + 1) * CHUNK)
        first = jnp.concatenate([lor[s, :, lanes]] * 4, axis=0)
        pos = c * CHUNK + iota((32, CHUNK), 1)
        one_back = first < pos
        two_back = first < pos - 1
        for r0 in range(0, 2 * WIDTH, 32):
            rows = slice(r0, r0 + 32)
            ext = qkv[s, rows, c * CHUNK:(c + 1) * CHUNK + 128]
            x1 = pltpu.roll(ext, 1, 1)[:, 128:]
            x2 = pltpu.roll(ext, 2, 1)[:, 128:]

            def tap(j):
                return jnp.concatenate([taps[j, rows, :]] * (CHUNK // 128), axis=1)

            m = tap(0) * ext[:, 128:]
            m = m + tap(1) * jnp.where(one_back, x1, 0.0)
            m = m + tap(2) * jnp.where(two_back, x2, 0.0)
            m = m.astype(bf16)
            h, d = r0 // WIDTH, r0 % WIDTH
            if d == 0:
                qkt[s, 32 * h:32 * h + 32, lanes] = m
            else:
                vv[2 * s + h, d - 32:d, lanes] = m

    def summarise(s, half):
        inside = begin_of(s, base + T - 1) - base
        W = T // 2
        at = half * W
        lanes = slice(at, at + W)
        for h in range(2):
            g = 2 * s + h
            key = qkt[s, 32 * h + FEAT:32 * h + 2 * FEAT, lanes].astype(f32)
            key = jnp.where(at + iota((FEAT, W), 1) >= inside, key, 0.0)
            small_key = key * (1.0 / 16.0)
            kd[g, 0:FEAT, lanes] = small_key
            kd[g, FEAT:2 * FEAT, lanes] = small_key
            blocks = [(key * kd[g, d:d + FEAT, lanes]).astype(bf16) for d in range(8)]
            here = (at + iota((8, W), 1) >= inside) & (iota((8, W), 0) == 0)
            last = [key[:8] * kd[g, 8:16, lanes], jnp.where(here, 0.125, 0.0)]
            blocks.append(jnp.concatenate(last, axis=0).astype(bf16))
            blocks.append((key * 0.125).astype(bf16))
            total = nt(jnp.concatenate(blocks, axis=0), vv[g, :, lanes])
            if half == 0:
                partial[g] = total
                continue
            total = partial[g] + total
            state, norm = total[:, :HEAD], total[:, HEAD:]
            f, l = iota((KEPT, HEAD), 0), iota((KEPT, HEAD), 1)
            n0 = jnp.sum(jnp.where(f == l, norm, 0.0), axis=0, keepdims=True)
            n1 = jnp.sum(jnp.where(f == l + HEAD, norm, 0.0), axis=0, keepdims=True)
            state = jnp.where(f == ZROW, n0, jnp.where(f == ZROW + 1, n1, state)).astype(bf16)
            lbuf[s, 2 * h] = state[:PIECE]
            lbuf[s, 2 * h + 1] = state[PIECE:]

    def p1(s, k):
        return pltpu.make_async_remote_copy(
            lbuf.at[s, lax.rem(y + k, ROW)], xbuf.at[s, k - 1], p1s.at[s, k - 1], p1r.at[s, k - 1],
            device_id=along_y(k), device_id_type=MESH)

    def p2(s, k):
        return pltpu.make_async_remote_copy(
            rsend.at[s], zbuf.at[s, k - 1], p2s.at[s, k - 1], p2r.at[s, k - 1],
            device_id=along_z(k), device_id_type=MESH)

    def p3(s, k):
        return pltpu.make_async_remote_copy(
            esend.at[s, k - 1], ebuf.at[s, y], p3s.at[s, k - 1], p3r.at[s, k - 1],
            device_id=along_y(k), device_id_type=MESH)

    def p3_in(s, k):
        return pltpu.make_async_remote_copy(
            esend.at[s, k - 1], ebuf.at[s, lax.rem(y - k + ROW, ROW)], p3s.at[s, k - 1], p3r.at[s, k - 1],
            device_id=along_y(k), device_id_type=MESH)

    def ss(s, k):
        return pltpu.make_async_remote_copy(
            ssb.at[s], ssr.at[s, k - 1], sss.at[s, k - 1], ssrs.at[s, k - 1],
            device_id=along_h(k), device_id_type=MESH)

    rowbase = z * (ROW * T)

    def last_of(j):
        return rowbase + (j + 1) * T - 1

    def gathered(s):
        parts = [lbuf[s, y].astype(f32)]
        owners = [y]
        for k in (1, 2, 3):
            parts.append(xbuf[s, k - 1].astype(f32))
            owners.append(lax.rem(y - k + ROW, ROW))
        return parts, owners

    def row_sum(s):
        for k in (1, 2, 3):
            p1(s, k).wait_recv()
        parts, owners = gathered(s)
        begin = begin_of(s, last_of(ROW - 1))
        total = jnp.zeros((PIECE, HEAD), f32)
        for part, j in zip(parts, owners):
            total = total + jnp.where(begin <= last_of(j), part, 0.0)
        rsend[s] = total.astype(bf16)
        for k in (1, 2):
            p2(s, k).start()

    def entering(s):
        for k in (1, 2):
            p2(s, k).wait_recv()
        parts, owners = gathered(s)
        one, two = zbuf[s, 0].astype(f32), zbuf[s, 1].astype(f32)
        for k in (1, 2, 3, 0):
            target = lax.rem(y + k, ROW)
            begin = begin_of(s, rowbase + target * T)
            total = jnp.where(begin < rowbase, one, 0.0) + jnp.where(begin < rowbase - ROW * T, two, 0.0)
            for part, j in zip(parts, owners):
                reach = jnp.where(j < target, last_of(j), -1)
                total = total + jnp.where(begin <= reach, part, 0.0)
            if k:
                esend[s, k - 1] = total.astype(bf16)
                p3(s, k).start()
            else:
                ebuf[s, y] = total.astype(bf16)

    def attend(s, h):
        g = 2 * s + h
        for c in range(C):
            rows = slice(c * CHUNK, (c + 1) * CHUNK)
            q = qk[s, rows, :]
            first = jnp.concatenate([loc[s, rows, :]] * (CHUNK // 128), axis=1)
            cols = iota((CHUNK, CHUNK), 1)
            parts = []
            for b in range(c + 1):
                u = nn(q, kk[g, :, b * CHUNK:(b + 1) * CHUNK])
                u = u * u + 0.0625
                keep = cols + b * CHUNK >= first
                if b == c:
                    keep = keep & (cols <= iota((CHUNK, CHUNK), 0))
                parts.append(jnp.where(keep, u, 0.0).astype(bf16))
            weights = parts[0] if c == 0 else jnp.concatenate(parts, axis=1)
            nd[g, rows, :] = nt(weights, vv[g, :, :(c + 1) * CHUNK])

    def queries(s, h):
        g = 2 * s + h
        for c in range(C):
            rows = slice(c * CHUNK, (c + 1) * CHUNK)
            ab = nn(qk[s, rows, :], eq[h])
            phq[g, rows, :] = (ab[:, :256] * ab[:, 256:]).astype(bf16)

    def turn(s):
        for r0 in range(0, T, 64):
            loc[s, r0:r0 + 64, :] = places(s, base + r0 + iota((64, 128), 0))
        same = jnp.where(iota((CHUNK, CHUNK), 0) == iota((CHUNK, CHUNK), 1), 1.0, 0.0).astype(bf16)
        for c in range(C):
            rows = slice(c * CHUNK, (c + 1) * CHUNK)
            qk[s, rows, :] = nt(same, qkt[s, :, rows]).astype(bf16)
        for h in range(2):
            kk[2 * s + h] = nn(mk[h], qkt[s]).astype(bf16)

    def finish(s):
        for k in (1, 2, 3):
            p3_in(s, k).wait_recv()
        rhs = []
        f, l = iota((KEPT, HEAD), 0), iota((KEPT, HEAD), 1)
        for h in range(2):
            state = jnp.concatenate([ebuf[s, 2 * h], ebuf[s, 2 * h + 1]], axis=0)
            wide = state.astype(f32)
            n0, n1 = wide[ZROW:ZROW + 1], wide[ZROW + 1:ZROW + 2]
            norm = jnp.sum(jnp.where(f == l, n0, 0.0) + jnp.where(f == l + HEAD, n1, 0.0), axis=1, keepdims=True)
            norm = jnp.broadcast_to(norm, (KEPT, HEAD)).astype(bf16)
            both = jnp.concatenate([state, norm], axis=1)
            rhs.append(jnp.concatenate([both, jnp.zeros((256 - KEPT, 256), bf16)], axis=0))
        eye = iota((128, 128), 0) == iota((128, 128), 1)
        for r0 in range(0, T, 128):
            rows = slice(r0, r0 + 128)
            use = loc[s, rows, :] < 0
            squares = jnp.zeros((128, 128), f32)
            for h in range(2):
                g = 2 * s + h
                came = nn(phq[g, rows, :], rhs[h])
                num = nd[g, rows, :HEAD] + jnp.where(use, came[:, :HEAD], 0.0)
                den = nd[g, rows, HEAD:] + jnp.where(use, came[:, HEAD:], 0.0)
                a = num / den
                att[s, rows, h * HEAD:(h + 1) * HEAD] = a
                squares = squares + a * a
            col = jnp.sum(squares, axis=1, keepdims=True)
            i = r0 // 128
            ssb[s, i:i + 1, :] = jnp.sum(jnp.where(eye, col, 0.0), axis=0, keepdims=True)
        for k in range(1, hn):
            ss(s, k).start()

    def scale(s):
        for k in range(1, hn):
            ss(s, k).wait_recv()
        total = ssb[s]
        for k in range(1, hn):
            total = total + ssr[s, k - 1]
        fac[s] = lax.rsqrt(total / (hn * 2 * HEAD) + 1e-06)

    def greet():
        pl.semaphore_wait(barrier, len(sources))

    def pieces_out(s):
        for k in (1, 2, 3):
            p1(s, k).start()

    def drain():
        rim.wait_send()
        for s in range(2):
            for k in (1, 2, 3):
                p1(s, k).wait_send()
                p3(s, k).wait_send()
            for k in (1, 2):
                p2(s, k).wait_send()
            for k in range(1, hn):
                ss(s, k).wait_send()

    L = C - 1
    plan = [(bounds,), (prepare,), (columns_in,)] + [(request, 0, c) for c in range(L)]
    plan += [(arrive, 0, L), (arrive, 1, L)] + [(request, 1, c) for c in range(L)] + [(tables_in,)]
    plan += [(project, 0, L, C), (project, 1, L, C), (greet,), (rim.start,)]
    plan += [(arrive, 0, c) for c in range(L)] + [(project, 0, 0, L)]
    plan += [(arrive, 1, c) for c in range(L)] + [(project, 1, 0, L)]
    plan += [(mix, 0, c) for c in range(1, C)] + [(mix, 1, c) for c in range(1, C)]
    plan += [(rim_in,), (mix, 0, 0), (summarise, 0, 0), (summarise, 0, 1), (pieces_out, 0)]
    plan += [(mix, 1, 0), (summarise, 1, 0), (summarise, 1, 1), (pieces_out, 1)]
    plan += [(ready,), (turn, 0), (turn, 1), (attend, 0, 0)]
    plan += [(row_sum, 0), (row_sum, 1), (attend, 0, 1), (attend, 1, 0)]
    plan += [(entering, 0), (entering, 1), (queries, 0, 0), (queries, 0, 1), (queries, 1, 0), (queries, 1, 1)]
    plan += [(attend, 1, 1), (finish, 0), (finish, 1), (scale, 0), (scale, 1), (drain,)]
    for step, *where in plan:
        step(*where)


def rescale(att, fac, gain, out, obuf, osem):
    T = att.shape[1]
    eye = iota((128, 128), 0) == iota((128, 128), 1)
    g = gain[...].astype(f32).reshape(1, 2 * HEAD)

    def write(s, c):
        rows = pl.ds(c * CHUNK, CHUNK)
        return pltpu.make_async_copy(obuf.at[s, rows], out.at[s, rows], osem.at[s, c])

    for s in range(2):
        for r0 in range(0, T, 128):
            i = r0 // 128
            rows = slice(r0, r0 + 128)
            col = jnp.sum(jnp.where(eye, fac[s, i:i + 1, :], 0.0), axis=1, keepdims=True)
            obuf[s, rows, :] = (att[s, rows, :] * col * g).astype(bf16)
            if (r0 + 128) % CHUNK == 0:
                write(s, r0 // CHUNK).start()
    for s in range(2):
        for c in range(T // CHUNK):
            write(s, c).wait()


def shards(zn, hn, hidden, w_qkv, conv_weight, norm_gain, repo_lengths):
    seqs, T, D = hidden.shape
    C = T // CHUNK
    query, move = tables()
    any_spec = pl.BlockSpec(memory_space=pl.ANY)
    vmem = pl.BlockSpec(memory_space=pltpu.VMEM)
    dma = pltpu.SemaphoreType.DMA

    def pin(x):
        return pltpu.with_memory_space_constraint(jnp.asarray(x), pltpu.HBM)

    att, fac = pl.pallas_call(
        functools.partial(kernel, zn, hn),
        out_shape=(jax.ShapeDtypeStruct((seqs, T, 2 * HEAD), f32), jax.ShapeDtypeStruct((seqs, T // 128, 128), f32)),
        in_specs=[any_spec] * 6,
        out_specs=(vmem, vmem),
        scratch_shapes=[
            pltpu.VMEM((2, T, D), bf16),
            pltpu.VMEM((2 * WIDTH, D), bf16),
            pltpu.VMEM(conv_weight.shape, f32),
            pltpu.SMEM(repo_lengths.shape, jnp.int32),
            pltpu.VMEM(query.shape, bf16),
            pltpu.VMEM(move.shape, bf16),
            pltpu.VMEM((3, 2 * WIDTH, 128), f32),
            pltpu.VMEM((4, 2 * FEAT, T), f32),
            pltpu.VMEM((4, KEPT, 256), f32),
            pltpu.VMEM((2, 2 * WIDTH, 128 + T), f32),
            pltpu.VMEM((2, 8, T), jnp.int32),
            pltpu.VMEM((2, T, 128), jnp.int32),
            pltpu.VMEM((2, 128, T), bf16),
            pltpu.VMEM((2, T, 128), bf16),
            pltpu.VMEM((4, 128, T), bf16),
            pltpu.VMEM((4, 256, T), bf16),
            pltpu.VMEM((4, T, 256), bf16),
            pltpu.VMEM((4, T, 256), f32),
            pltpu.VMEM((2, RIM, 2 * WIDTH), bf16),
            pltpu.VMEM((2, RIM, 2 * WIDTH), bf16),
            pltpu.VMEM((2, ROW, PIECE, HEAD), bf16),
            pltpu.VMEM((2, 3, PIECE, HEAD), bf16),
            pltpu.VMEM((2, PIECE, HEAD), bf16),
            pltpu.VMEM((2, 2, PIECE, HEAD), bf16),
            pltpu.VMEM((2, 3, PIECE, HEAD), bf16),
            pltpu.VMEM((2, ROW, PIECE, HEAD), bf16),
            pltpu.VMEM((2, T // 128, 128), f32),
            pltpu.VMEM((2, max(hn - 1, 1), T // 128, 128), f32),
            dma,
            dma((4,)),
            dma((2, C)),
            dma((2,)),
            dma((2, 3)),
            dma((2, 3)),
            dma((2, 2)),
            dma((2, 2)),
            dma((2, 3)),
            dma((2, 3)),
            dma((2, max(hn - 1, 1))),
            dma((2, max(hn - 1, 1))),
        ],
        compiler_params=pltpu.CompilerParams(
            collective_id=0, has_side_effects=True, vmem_limit_bytes=44 * 1024 * 1024),
        name="packed_linear_attention",
    )(pin(hidden), pin(w_qkv.T), pin(conv_weight), pin(repo_lengths), pin(query), pin(move))
    return pl.pallas_call(
        rescale,
        out_shape=jax.ShapeDtypeStruct((seqs, T, 2 * HEAD), bf16),
        in_specs=[vmem, vmem, vmem],
        out_specs=any_spec,
        scratch_shapes=[pltpu.VMEM((2, T, 2 * HEAD), bf16), dma((2, C))],
        compiler_params=pltpu.CompilerParams(vmem_limit_bytes=8 * 1024 * 1024),
        name="rescale_rows",
    )(att, fac, norm_gain)


def solution(mesh):
    zn, hn = mesh.shape["seq"] // ROW, mesh.shape["head"]
    in_specs = (P(None, "seq", None), P(None, "head"), P(None, "head"), P("head"), P())
    out_specs = P(None, "seq", "head")
    return jax.shard_map(
        functools.partial(shards, zn, hn), mesh=mesh, in_specs=in_specs, out_specs=out_specs, check_vma=False)
```

```python
import functools
import jax
import jax.numpy as jnp
import numpy as np
from jax import lax
from jax.experimental import pallas as pl
from jax.experimental.pallas import tpu as pltpu
from jax.sharding import PartitionSpec as P

FEAT = 16
HEAD = 128
WIDTH = 2 * FEAT + HEAD
NSEG = 12
ROW = 4
CHUNK = 256
RIM = 16
KEPT = 160
PIECE = 80
ONE = 64
QUAD = 136
ZROW = 137
LINEAR = 144
MESH = pl.DeviceIdType.MESH
bf16 = jnp.bfloat16
f32 = jnp.float32


def tables():
    query = np.zeros((2, 128, 512), np.float32)
    move = np.zeros((2, 128, 128), np.float32)
    for h in range(2):
        qb, kb = 32 * h, 32 * h + FEAT
        for f in range(QUAD):
            d, i = f // FEAT, f % FEAT
            query[h, qb + i, f] = 1 / 8 if d else 1 / 16
            query[h, qb + (i + d) % FEAT, 256 + f] = 1.0
        query[h, ONE, QUAD] = 1.0
        query[h, ONE, 256 + QUAD] = 1.0
        for i in range(FEAT):
            query[h, qb + i, LINEAR + i] = 1 / 4
            query[h, ONE, 256 + LINEAR + i] = 1.0
            move[h, qb + i, kb + i] = 1 / 16
        move[h, ONE, ONE] = 1 / 4
    return query.astype(jnp.bfloat16), move.astype(jnp.bfloat16)


def nt(a, b):
    return lax.dot_general(a, b, (((1,), (1,)), ((), ())), preferred_element_type=f32)


def nn(a, b):
    return jnp.dot(a, b, preferred_element_type=f32)


def iota(shape, dim):
    return lax.broadcasted_iota(jnp.int32, shape, dim)


def kernel(zn, hn, hid, wq, conv_in, lengths_in, eq_in, mk_in, att, fac,
           hbuf, wbuf, conv, lengths, eq, mk, taps, kd, partial, qkv, lor, loc, qkt, qk, kk, vv, phq, nd, rim_s, rim_r, lbuf, xbuf,
           rsend, zbuf, esend, ebuf, inrow, ssb, ssr,
           wsem, csem, hsem, rim_sem, p1s, p1r, p2s, p2r, p3s, p3r, sss, ssrs):
    T = hbuf.shape[1]
    C = T // CHUNK
    G = T // 128
    me = lax.axis_index("seq")
    hd = lax.axis_index("head")
    z = me // ROW
    y = lax.rem(me, ROW)

    def at_seq(i):
        return (i, hd)

    def along_y(k):
        return (z * ROW + lax.rem(y + k + ROW, ROW), hd)

    def along_z(k):
        return (lax.rem(z + k + zn, zn) * ROW + y, hd)

    def along_h(k):
        return (me, lax.rem(hd + k + hn, hn))

    nxt = at_seq(lax.rem(me + 1, zn * ROW))
    prv = at_seq(lax.rem(me + zn * ROW - 1, zn * ROW))

    wcopy = pltpu.make_async_copy(wq, wbuf, wsem)

    def small(i):
        source, target = ((lengths_in, lengths), (conv_in, conv), (mk_in, mk), (eq_in, eq))[i]
        return pltpu.make_async_copy(source, target, csem.at[i])

    small(0).start()
    small(1).start()
    wcopy.start()
    def fetch(s, c):
        rows = pl.ds(c * CHUNK, CHUNK)
        return pltpu.make_async_copy(hid.at[s, rows], hbuf.at[s, rows], hsem.at[s, c])

    def request(s, c):
        fetch(s, c).start()

    request(0, C - 1)
    request(1, C - 1)

    barrier = pltpu.get_barrier_semaphore()
    sources = [prv] + [along_y(-k) for k in (1, 2, 3)] + [along_z(-k) for k in (1, 2)]
    sources += [along_h(-k) for k in range(1, hn)]
    for d in sources:
        pl.semaphore_signal(barrier, inc=1, device_id=d, device_id_type=MESH)

    starts = []

    def bounds():
        small(0).wait()
        for s in range(2):
            run = jnp.int32(0)
            own = []
            for r in range(NSEG - 1):
                run = run + lengths[s, r]
                own.append(run)
            starts.append(own)

    def begin_of(s, t):
        found = jnp.int32(0)
        for b in starts[s]:
            found = jnp.where(b <= t, b, found)
        return found

    base = me * T

    def places(s, pos):
        found = jnp.zeros(pos.shape, jnp.int32)
        for b in starts[s]:
            found = jnp.where(pos >= b, b, found)
        return found - base

    def prepare():
        for s in range(2):
            lor[s] = places(s, base + iota((8, T), 1))
            qkt[s, ONE:ONE + 16, :] = jnp.where(iota((16, T), 0) == 0, 1.0, 0.0).astype(bf16)
            qkt[s, ONE + 16:, :] = jnp.zeros((128 - ONE - 16, T), bf16)
            for h in range(2):
                vv[2 * s + h, HEAD:, :] = jnp.ones((HEAD, T), bf16)
        small(1).wait()
        for j in range(3):
            for c0 in range(0, 2 * WIDTH, 64):
                row = jnp.broadcast_to(conv[j:j + 1, c0:c0 + 64], (64, 64))
                eye = iota((64, 64), 0) == iota((64, 64), 1)
                col = jnp.sum(jnp.where(eye, row, 0.0), axis=1, keepdims=True)
                taps[j, c0:c0 + 64, :] = jnp.broadcast_to(col, (64, 128))

    def ready():
        for i in range(2, 4):
            small(i).wait()

    def tables_in():
        for i in range(2, 4):
            small(i).start()

    def columns_in():
        wcopy.wait()

    def arrive(s, c):
        fetch(s, c).wait()

    def project(s, low_c, high_c):
        rows = slice(low_c * CHUNK, high_c * CHUNK)
        low = nt(wbuf[...], hbuf[s, rows, :]).astype(bf16)
        qkv[s, :, 128 + low_c * CHUNK:128 + high_c * CHUNK] = low.astype(f32)
        if high_c == C:
            pick = jnp.where(iota((RIM, 128), 1) == iota((RIM, 128), 0) + 128 - RIM, 1.0, 0.0).astype(bf16)
            rim_s[s] = nt(pick, low[:, low.shape[1] - 128:]).astype(bf16)

    rim = pltpu.make_async_remote_copy(rim_s, rim_r, rim_sem.at[0], rim_sem.at[1], device_id=nxt, device_id_type=MESH)

    def rim_in():
        rim.wait_recv()
        pick = jnp.where(iota((RIM, 128), 1) == iota((RIM, 128), 0) + 128 - RIM, 1.0, 0.0).astype(bf16)
        for s in range(2):
            qkv[s, :, 0:128] = lax.dot_general(
                rim_r[s], pick, (((0,), (0,)), ((), ())), preferred_element_type=f32)

    def mix(s, c):
        lanes = slice(c * CHUNK, (c + 1) * CHUNK)
        first = jnp.concatenate([lor[s, :, lanes]] * 4, axis=0)
        pos = c * CHUNK + iota((32, CHUNK), 1)
        one_back = first < pos
        two_back = first < pos - 1
        for r0 in range(0, 2 * WIDTH, 32):
            rows = slice(r0, r0 + 32)
            ext = qkv[s, rows, c * CHUNK:(c + 1) * CHUNK + 128]
            x1 = pltpu.roll(ext, 1, 1)[:, 128:]
            x2 = pltpu.roll(ext, 2, 1)[:, 128:]

            def tap(j):
                return jnp.concatenate([taps[j, rows, :]] * (CHUNK // 128), axis=1)

            m = tap(0) * ext[:, 128:]
            m = m + tap(1) * jnp.where(one_back, x1, 0.0)
            m = m + tap(2) * jnp.where(two_back, x2, 0.0)
            m = m.astype(bf16)
            h, d = r0 // WIDTH, r0 % WIDTH
            if d == 0:
                qkt[s, 32 * h:32 * h + 32, lanes] = m
            else:
                vv[2 * s + h, d - 32:d, lanes] = m

    def summarise(s, half):
        inside = begin_of(s, base + T - 1) - base
        W = T // 2
        at = half * W
        lanes = slice(at, at + W)
        for h in range(2):
            g = 2 * s + h
            key = qkt[s, 32 * h + FEAT:32 * h + 2 * FEAT, lanes].astype(f32)
            key = jnp.where(at + iota((FEAT, W), 1) >= inside, key, 0.0)
            small_key = key * (1.0 / 16.0)
            kd[g, 0:FEAT, lanes] = small_key
            kd[g, FEAT:2 * FEAT, lanes] = small_key
            blocks = [(key * kd[g, d:d + FEAT, lanes]).astype(bf16) for d in range(8)]
            here = (at + iota((8, W), 1) >= inside) & (iota((8, W), 0) == 0)
            last = [key[:8] * kd[g, 8:16, lanes], jnp.where(here, 0.125, 0.0)]
            blocks.append(jnp.concatenate(last, axis=0).astype(bf16))
            blocks.append((key * 0.125).astype(bf16))
            total = nt(jnp.concatenate(blocks, axis=0), vv[g, :, lanes])
            if half == 0:
                partial[g] = total
                continue
            total = partial[g] + total
            state, norm = total[:, :HEAD], total[:, HEAD:]
            f, l = iota((KEPT, HEAD), 0), iota((KEPT, HEAD), 1)
            n0 = jnp.sum(jnp.where(f == l, norm, 0.0), axis=0, keepdims=True)
            n1 = jnp.sum(jnp.where(f == l + HEAD, norm, 0.0), axis=0, keepdims=True)
            state = jnp.where(f == ZROW, n0, jnp.where(f == ZROW + 1, n1, state)).astype(bf16)
            lbuf[2 * h, s] = state[:PIECE]
            lbuf[2 * h + 1, s] = state[PIECE:]

    def p1(k):
        return pltpu.make_async_remote_copy(
            lbuf.at[lax.rem(y + k, ROW)], xbuf.at[k - 1], p1s.at[k - 1], p1r.at[k - 1],
            device_id=along_y(k), device_id_type=MESH)

    def p2(k):
        return pltpu.make_async_remote_copy(
            rsend, zbuf.at[k - 1], p2s.at[k - 1], p2r.at[k - 1],
            device_id=along_z(k), device_id_type=MESH)

    def p3(k):
        return pltpu.make_async_remote_copy(
            esend.at[k - 1], ebuf.at[y], p3s.at[k - 1], p3r.at[k - 1],
            device_id=along_y(k), device_id_type=MESH)

    def p3_in(k):
        return pltpu.make_async_remote_copy(
            esend.at[k - 1], ebuf.at[lax.rem(y - k + ROW, ROW)], p3s.at[k - 1], p3r.at[k - 1],
            device_id=along_y(k), device_id_type=MESH)

    def ss(k):
        return pltpu.make_async_remote_copy(
            ssb, ssr.at[k - 1], sss.at[k - 1], ssrs.at[k - 1],
            device_id=along_h(k), device_id_type=MESH)

    rowbase = z * (ROW * T)
    owners = [y] + [lax.rem(y - k + ROW, ROW) for k in (1, 2, 3)]

    def last_of(j):
        return rowbase + (j + 1) * T - 1

    def gathered(s):
        return [lbuf[y, s].astype(f32)] + [xbuf[k - 1, s].astype(f32) for k in (1, 2, 3)]

    def row_sum():
        keep = []
        for s in range(2):
            begin = begin_of(s, last_of(ROW - 1))
            keep.append([begin <= last_of(j) for j in owners])
        for k in (1, 2, 3):
            p1(k).wait_recv()
        for s in range(2):
            total = jnp.zeros((PIECE, HEAD), f32)
            for part, on in zip(gathered(s), keep[s]):
                total = total + jnp.where(on, part, 0.0)
            rsend[s] = total.astype(bf16)
        for k in (2, 1):
            p2(k).start()
        for k in (1, 2, 3, 0):
            target = lax.rem(y + k, ROW)
            for s in range(2):
                begin = begin_of(s, rowbase + target * T)
                total = jnp.zeros((PIECE, HEAD), f32)
                for part, j in zip(gathered(s), owners):
                    reach = jnp.where(j < target, last_of(j), -1)
                    total = total + jnp.where(begin <= reach, part, 0.0)
                inrow[k, s] = total

    def entering():
        reach = {}
        for k in range(4):
            target = lax.rem(y + k, ROW)
            for s in range(2):
                begin = begin_of(s, rowbase + target * T)
                reach[k, s] = (begin < rowbase, begin < rowbase - ROW * T)
        for k in (1, 2):
            p2(k).wait_recv()
        for k in (2, 1, 3, 0):
            for s in range(2):
                near, far = reach[k, s]
                total = inrow[k, s] + jnp.where(near, zbuf[0, s].astype(f32), 0.0)
                total = (total + jnp.where(far, zbuf[1, s].astype(f32), 0.0)).astype(bf16)
                if k:
                    esend[k - 1, s] = total
                else:
                    ebuf[y, s] = total
            if k:
                p3(k).start()

    def attend(s, h):
        g = 2 * s + h
        for c in range(C):
            rows = slice(c * CHUNK, (c + 1) * CHUNK)
            q = qk[s, rows, :]
            first = jnp.concatenate([loc[s, rows, :]] * (CHUNK // 128), axis=1)
            cols = iota((CHUNK, CHUNK), 1)
            parts = []
            for b in range(c + 1):
                u = nn(q, kk[g, :, b * CHUNK:(b + 1) * CHUNK])
                u = u * u + 0.0625
                keep = cols + b * CHUNK >= first
                if b == c:
                    keep = keep & (cols <= iota((CHUNK, CHUNK), 0))
                parts.append(jnp.where(keep, u, 0.0).astype(bf16))
            weights = parts[0] if c == 0 else jnp.concatenate(parts, axis=1)
            nd[g, rows, :] = nt(weights, vv[g, :, :(c + 1) * CHUNK])

    def queries(s, h):
        g = 2 * s + h
        for c in range(C):
            rows = slice(c * CHUNK, (c + 1) * CHUNK)
            ab = nn(qk[s, rows, :], eq[h])
            phq[g, rows, :] = (ab[:, :256] * ab[:, 256:]).astype(bf16)

    def turn(s):
        for r0 in range(0, T, 64):
            loc[s, r0:r0 + 64, :] = places(s, base + r0 + iota((64, 128), 0))
        same = jnp.where(iota((CHUNK, CHUNK), 0) == iota((CHUNK, CHUNK), 1), 1.0, 0.0).astype(bf16)
        for c in range(C):
            rows = slice(c * CHUNK, (c + 1) * CHUNK)
            qk[s, rows, :] = nt(same, qkt[s, :, rows]).astype(bf16)
        for h in range(2):
            kk[2 * s + h] = nn(mk[h], qkt[s]).astype(bf16)

    def entered():
        for k in (1, 2, 3):
            p3_in(k).wait_recv()

    def finish(s):
        rhs = []
        f, l = iota((KEPT, HEAD), 0), iota((KEPT, HEAD), 1)
        for h in range(2):
            state = jnp.concatenate([ebuf[2 * h, s], ebuf[2 * h + 1, s]], axis=0)
            wide = state.astype(f32)
            n0, n1 = wide[ZROW:ZROW + 1], wide[ZROW + 1:ZROW + 2]
            norm = jnp.sum(jnp.where(f == l, n0, 0.0) + jnp.where(f == l + HEAD, n1, 0.0), axis=1, keepdims=True)
            norm = jnp.broadcast_to(norm, (KEPT, HEAD)).astype(bf16)
            both = jnp.concatenate([state, norm], axis=1)
            rhs.append(jnp.concatenate([both, jnp.zeros((256 - KEPT, 256), bf16)], axis=0))
        eye = iota((128, 128), 0) == iota((128, 128), 1)
        for r0 in range(0, T, 128):
            rows = slice(r0, r0 + 128)
            use = loc[s, rows, :] < 0
            squares = jnp.zeros((128, 128), f32)
            for h in range(2):
                g = 2 * s + h
                came = nn(phq[g, rows, :], rhs[h])
                num = nd[g, rows, :HEAD] + jnp.where(use, came[:, :HEAD], 0.0)
                den = nd[g, rows, HEAD:] + jnp.where(use, came[:, HEAD:], 0.0)
                a = num / den
                att[s, rows, h * HEAD:(h + 1) * HEAD] = a
                squares = squares + a * a
            col = jnp.sum(squares, axis=1, keepdims=True)
            i = r0 // 128
            ssb[s, i:i + 1, :] = jnp.sum(jnp.where(eye, col, 0.0), axis=0, keepdims=True)

    peers = sorted(range(1, hn), key=lambda k: -min(k, hn - k))

    def squares_out():
        for k in peers:
            ss(k).start()

    def scale():
        for k in peers:
            ss(k).wait_recv()
        total = ssb[...]
        for k in range(1, hn):
            total = total + ssr[k - 1]
        fac[...] = lax.rsqrt(total / (hn * 2 * HEAD) + 1e-06)

    def greet():
        pl.semaphore_wait(barrier, len(sources))

    def pieces_out():
        for k in (2, 1, 3):
            p1(k).start()

    def drain():
        rim.wait_send()
        for k in (1, 2, 3):
            p1(k).wait_send()
            p3(k).wait_send()
        for k in (1, 2):
            p2(k).wait_send()
        for k in peers:
            ss(k).wait_send()

    L = C - 1
    plan = [(bounds,), (prepare,), (columns_in,)] + [(request, 0, c) for c in range(L)]
    plan += [(arrive, 0, L), (arrive, 1, L)] + [(request, 1, c) for c in range(L)] + [(tables_in,)]
    plan += [(project, 0, L, C), (project, 1, L, C), (greet,), (rim.start,)]
    plan += [(arrive, 0, c) for c in range(L)] + [(project, 0, 0, L)]
    plan += [(arrive, 1, c) for c in range(L)] + [(project, 1, 0, L)]
    plan += [(mix, 0, c) for c in range(1, C)] + [(mix, 1, c) for c in range(1, C)]
    plan += [(rim_in,), (mix, 0, 0), (summarise, 0, 0), (summarise, 0, 1)]
    plan += [(mix, 1, 0), (summarise, 1, 0), (summarise, 1, 1), (pieces_out,)]
    plan += [(ready,), (turn, 0), (turn, 1), (attend, 0, 0), (row_sum,), (attend, 0, 1), (attend, 1, 0), (entering,)]
    plan += [(queries, s, h) for s in range(2) for h in range(2)] + [(attend, 1, 1), (entered,)]
    plan += [(finish, 0), (finish, 1), (squares_out,), (scale,), (drain,)]
    for step, *where in plan:
        step(*where)


def rescale(att, fac, gain, out, obuf, osem):
    T = att.shape[1]
    eye = iota((128, 128), 0) == iota((128, 128), 1)
    g = gain[...].astype(f32).reshape(1, 2 * HEAD)

    def write(s, c):
        rows = pl.ds(c * CHUNK, CHUNK)
        return pltpu.make_async_copy(obuf.at[s, rows], out.at[s, rows], osem.at[s, c])

    for s in range(2):
        for r0 in range(0, T, 128):
            i = r0 // 128
            rows = slice(r0, r0 + 128)
            col = jnp.sum(jnp.where(eye, fac[s, i:i + 1, :], 0.0), axis=1, keepdims=True)
            obuf[s, rows, :] = (att[s, rows, :] * col * g).astype(bf16)
            if (r0 + 128) % CHUNK == 0:
                write(s, r0 // CHUNK).start()
    for s in range(2):
        for c in range(T // CHUNK):
            write(s, c).wait()


def shards(zn, hn, hidden, w_qkv, conv_weight, norm_gain, repo_lengths):
    seqs, T, D = hidden.shape
    C = T // CHUNK
    query, move = tables()
    any_spec = pl.BlockSpec(memory_space=pl.ANY)
    vmem = pl.BlockSpec(memory_space=pltpu.VMEM)
    dma = pltpu.SemaphoreType.DMA

    def pin(x):
        return pltpu.with_memory_space_constraint(jnp.asarray(x), pltpu.HBM)

    att, fac = pl.pallas_call(
        functools.partial(kernel, zn, hn),
        out_shape=(jax.ShapeDtypeStruct((seqs, T, 2 * HEAD), f32), jax.ShapeDtypeStruct((seqs, T // 128, 128), f32)),
        in_specs=[any_spec] * 6,
        out_specs=(vmem, vmem),
        scratch_shapes=[
            pltpu.VMEM((2, T, D), bf16),
            pltpu.VMEM((2 * WIDTH, D), bf16),
            pltpu.VMEM(conv_weight.shape, f32),
            pltpu.SMEM(repo_lengths.shape, jnp.int32),
            pltpu.VMEM(query.shape, bf16),
            pltpu.VMEM(move.shape, bf16),
            pltpu.VMEM((3, 2 * WIDTH, 128), f32),
            pltpu.VMEM((4, 2 * FEAT, T), f32),
            pltpu.VMEM((4, KEPT, 256), f32),
            pltpu.VMEM((2, 2 * WIDTH, 128 + T), f32),
            pltpu.VMEM((2, 8, T), jnp.int32),
            pltpu.VMEM((2, T, 128), jnp.int32),
            pltpu.VMEM((2, 128, T), bf16),
            pltpu.VMEM((2, T, 128), bf16),
            pltpu.VMEM((4, 128, T), bf16),
            pltpu.VMEM((4, 256, T), bf16),
            pltpu.VMEM((4, T, 256), bf16),
            pltpu.VMEM((4, T, 256), f32),
            pltpu.VMEM((2, RIM, 2 * WIDTH), bf16),
            pltpu.VMEM((2, RIM, 2 * WIDTH), bf16),
            pltpu.VMEM((ROW, 2, PIECE, HEAD), bf16),
            pltpu.VMEM((3, 2, PIECE, HEAD), bf16),
            pltpu.VMEM((2, PIECE, HEAD), bf16),
            pltpu.VMEM((2, 2, PIECE, HEAD), bf16),
            pltpu.VMEM((3, 2, PIECE, HEAD), bf16),
            pltpu.VMEM((ROW, 2, PIECE, HEAD), bf16),
            pltpu.VMEM((4, 2, PIECE, HEAD), f32),
            pltpu.VMEM((2, T // 128, 128), f32),
            pltpu.VMEM((hn - 1, 2, T // 128, 128), f32),
            dma,
            dma((4,)),
            dma((2, C)),
            dma((2,)),
            dma((3,)),
            dma((3,)),
            dma((2,)),
            dma((2,)),
            dma((3,)),
            dma((3,)),
            dma((hn - 1,)),
            dma((hn - 1,)),
        ],
        compiler_params=pltpu.CompilerParams(
            collective_id=0, has_side_effects=True, vmem_limit_bytes=44 * 1024 * 1024),
        name="packed_linear_attention",
    )(pin(hidden), pin(w_qkv.T), pin(conv_weight), pin(repo_lengths), pin(query), pin(move))
    return pl.pallas_call(
        rescale,
        out_shape=jax.ShapeDtypeStruct((seqs, T, 2 * HEAD), bf16),
        in_specs=[vmem, vmem, vmem],
        out_specs=any_spec,
        scratch_shapes=[pltpu.VMEM((2, T, 2 * HEAD), bf16), dma((2, C))],
        compiler_params=pltpu.CompilerParams(vmem_limit_bytes=8 * 1024 * 1024),
        name="rescale_rows",
    )(att, fac, norm_gain)


def solution(mesh):
    zn, hn = mesh.shape["seq"] // ROW, mesh.shape["head"]
    in_specs = (P(None, "seq", None), P(None, "head"), P(None, "head"), P("head"), P())
    out_specs = P(None, "seq", "head")
    return jax.shard_map(
        functools.partial(shards, zn, hn), mesh=mesh, in_specs=in_specs, out_specs=out_specs, check_vma=False)
```

```python
import functools
import jax
import jax.numpy as jnp
import numpy as np
from jax import lax
from jax.experimental import pallas as pl
from jax.experimental.pallas import tpu as pltpu
from jax.sharding import PartitionSpec as P

FEAT = 16
HEAD = 128
WIDTH = 2 * FEAT + HEAD
NSEG = 12
ROW = 4
CHUNK = 256
RIM = 16
KEPT = 160
PIECE = 80
ONE = 64
QUAD = 136
ZROW = 137
LINEAR = 144
MESH = pl.DeviceIdType.MESH
bf16 = jnp.bfloat16
f32 = jnp.float32


def tables():
    query = np.zeros((2, 128, 512), np.float32)
    move = np.zeros((2, 128, 128), np.float32)
    for h in range(2):
        qb, kb = 32 * h, 32 * h + FEAT
        for f in range(QUAD):
            d, i = f // FEAT, f % FEAT
            query[h, qb + i, f] = 1 / 8 if d else 1 / 16
            query[h, qb + (i + d) % FEAT, 256 + f] = 1.0
        query[h, ONE, QUAD] = 1.0
        query[h, ONE, 256 + QUAD] = 1.0
        for i in range(FEAT):
            query[h, qb + i, LINEAR + i] = 1 / 4
            query[h, ONE, 256 + LINEAR + i] = 1.0
            move[h, qb + i, kb + i] = 1 / 16
        move[h, ONE, ONE] = 1 / 4
    return query.astype(jnp.bfloat16), move.astype(jnp.bfloat16)


def nt(a, b):
    return lax.dot_general(a, b, (((1,), (1,)), ((), ())), preferred_element_type=f32)


def nn(a, b):
    return jnp.dot(a, b, preferred_element_type=f32)


def iota(shape, dim):
    return lax.broadcasted_iota(jnp.int32, shape, dim)


def kernel(zn, hn, hid, wq, conv_in, lengths_in, eq_in, mk_in, att, fac,
           hbuf, wbuf, conv, lengths, eq, mk, taps, kd, partial, qkv, lor, loc, qkt, qk, kk, vv, phq, nd, rim_s, rim_r, lbuf, xbuf,
           rsend, zbuf, esend, ebuf, inrow, ssb, ssr,
           wsem, csem, hsem, rim_sem, p1s, p1r, p2s, p2r, p3s, p3r, sss, ssrs):
    T = hbuf.shape[1]
    C = T // CHUNK
    G = T // 128
    me = lax.axis_index("seq")
    hd = lax.axis_index("head")
    z = me // ROW
    y = lax.rem(me, ROW)

    def at_seq(i):
        return (i, hd)

    def along_y(k):
        return (z * ROW + lax.rem(y + k + ROW, ROW), hd)

    def along_z(k):
        return (lax.rem(z + k + zn, zn) * ROW + y, hd)

    def along_h(k):
        return (me, lax.rem(hd + k + hn, hn))

    nxt = at_seq(lax.rem(me + 1, zn * ROW))
    prv = at_seq(lax.rem(me + zn * ROW - 1, zn * ROW))

    wcopy = pltpu.make_async_copy(wq, wbuf, wsem)

    def small(i):
        source, target = ((lengths_in, lengths), (conv_in, conv), (mk_in, mk), (eq_in, eq))[i]
        return pltpu.make_async_copy(source, target, csem.at[i])

    small(0).start()
    small(1).start()
    wcopy.start()
    def fetch(s, c):
        rows = pl.ds(c * CHUNK, CHUNK)
        return pltpu.make_async_copy(hid.at[s, rows], hbuf.at[s, rows], hsem.at[s, c])

    def request(s, c):
        fetch(s, c).start()

    request(0, C - 1)
    request(1, C - 1)

    barrier = pltpu.get_barrier_semaphore()
    sources = [prv] + [along_y(-k) for k in (1, 2, 3)] + [along_z(-k) for k in (1, 2)]
    sources += [along_h(-k) for k in range(1, hn)]
    for d in sources:
        pl.semaphore_signal(barrier, inc=1, device_id=d, device_id_type=MESH)

    starts = []

    def bounds():
        small(0).wait()
        for s in range(2):
            run = jnp.int32(0)
            own = []
            for r in range(NSEG - 1):
                run = run + lengths[s, r]
                own.append(run)
            starts.append(own)

    def begin_of(s, t):
        found = jnp.int32(0)
        for b in starts[s]:
            found = jnp.where(b <= t, b, found)
        return found

    base = me * T

    def places(s, pos):
        found = jnp.zeros(pos.shape, jnp.int32)
        for b in starts[s]:
            found = jnp.where(pos >= b, b, found)
        return found - base

    def prepare():
        for s in range(2):
            lor[s] = places(s, base + iota((8, T), 1))
            qkt[s, ONE:ONE + 16, :] = jnp.where(iota((16, T), 0) == 0, 1.0, 0.0).astype(bf16)
            qkt[s, ONE + 16:, :] = jnp.zeros((128 - ONE - 16, T), bf16)
            for h in range(2):
                vv[2 * s + h, HEAD:, :] = jnp.ones((HEAD, T), bf16)
        small(1).wait()
        for j in range(3):
            for c0 in range(0, 2 * WIDTH, 64):
                row = jnp.broadcast_to(conv[j:j + 1, c0:c0 + 64], (64, 64))
                eye = iota((64, 64), 0) == iota((64, 64), 1)
                col = jnp.sum(jnp.where(eye, row, 0.0), axis=1, keepdims=True)
                taps[j, c0:c0 + 64, :] = jnp.broadcast_to(col, (64, 128))

    def ready():
        for i in range(2, 4):
            small(i).wait()

    def tables_in():
        for i in range(2, 4):
            small(i).start()

    def columns_in():
        wcopy.wait()

    def arrive(s, c):
        fetch(s, c).wait()

    def project(s, low_c, high_c):
        rows = slice(low_c * CHUNK, high_c * CHUNK)
        low = nt(wbuf[...], hbuf[s, rows, :]).astype(bf16)
        qkv[s, :, 128 + low_c * CHUNK:128 + high_c * CHUNK] = low.astype(f32)
        if high_c == C:
            pick = jnp.where(iota((RIM, 128), 1) == iota((RIM, 128), 0) + 128 - RIM, 1.0, 0.0).astype(bf16)
            rim_s[s] = nt(pick, low[:, low.shape[1] - 128:]).astype(bf16)

    rim = pltpu.make_async_remote_copy(rim_s, rim_r, rim_sem.at[0], rim_sem.at[1], device_id=nxt, device_id_type=MESH)

    def rim_in():
        rim.wait_recv()
        pick = jnp.where(iota((RIM, 128), 1) == iota((RIM, 128), 0) + 128 - RIM, 1.0, 0.0).astype(bf16)
        for s in range(2):
            qkv[s, :, 0:128] = lax.dot_general(
                rim_r[s], pick, (((0,), (0,)), ((), ())), preferred_element_type=f32)

    def mix(s, low, high):
        lanes = slice(low, high)
        first = jnp.concatenate([lor[s, :, lanes]] * 4, axis=0)
        pos = low + iota((32, high - low), 1)
        one_back = first < pos
        two_back = first < pos - 1
        for r0 in range(0, 2 * WIDTH, 32):
            rows = slice(r0, r0 + 32)
            ext = qkv[s, rows, low:high + 128]
            x1 = pltpu.roll(ext, 1, 1)[:, 128:]
            x2 = pltpu.roll(ext, 2, 1)[:, 128:]

            def tap(j):
                return jnp.concatenate([taps[j, rows, :]] * ((high - low) // 128), axis=1)

            m = tap(0) * ext[:, 128:]
            m = m + tap(1) * jnp.where(one_back, x1, 0.0)
            m = m + tap(2) * jnp.where(two_back, x2, 0.0)
            m = m.astype(bf16)
            h, d = r0 // WIDTH, r0 % WIDTH
            if d == 0:
                qkt[s, 32 * h:32 * h + 32, lanes] = m
            else:
                vv[2 * s + h, d - 32:d, lanes] = m

    def summarise(s, at, until):
        inside = begin_of(s, base + T - 1) - base
        W = until - at
        lanes = slice(at, until)
        for h in range(2):
            g = 2 * s + h
            key = qkt[s, 32 * h + FEAT:32 * h + 2 * FEAT, lanes].astype(f32)
            key = jnp.where(at + iota((FEAT, W), 1) >= inside, key, 0.0)
            small_key = key * (1.0 / 16.0)
            kd[g, 0:FEAT, lanes] = small_key
            kd[g, FEAT:2 * FEAT, lanes] = small_key
            blocks = [(key * kd[g, d:d + FEAT, lanes]).astype(bf16) for d in range(8)]
            here = (at + iota((8, W), 1) >= inside) & (iota((8, W), 0) == 0)
            last = [key[:8] * kd[g, 8:16, lanes], jnp.where(here, 0.125, 0.0)]
            blocks.append(jnp.concatenate(last, axis=0).astype(bf16))
            blocks.append((key * 0.125).astype(bf16))
            total = nt(jnp.concatenate(blocks, axis=0), vv[g, :, lanes])
            if at:
                partial[g] = total
                continue
            total = partial[g] + total
            state, norm = total[:, :HEAD], total[:, HEAD:]
            f, l = iota((KEPT, HEAD), 0), iota((KEPT, HEAD), 1)
            n0 = jnp.sum(jnp.where(f == l, norm, 0.0), axis=0, keepdims=True)
            n1 = jnp.sum(jnp.where(f == l + HEAD, norm, 0.0), axis=0, keepdims=True)
            state = jnp.where(f == ZROW, n0, jnp.where(f == ZROW + 1, n1, state)).astype(bf16)
            lbuf[2 * h, s] = state[:PIECE]
            lbuf[2 * h + 1, s] = state[PIECE:]

    def p1(k):
        return pltpu.make_async_remote_copy(
            lbuf.at[lax.rem(y + k, ROW)], xbuf.at[k - 1], p1s.at[k - 1], p1r.at[k - 1],
            device_id=along_y(k), device_id_type=MESH)

    def p2(k):
        return pltpu.make_async_remote_copy(
            rsend, zbuf.at[k - 1], p2s.at[k - 1], p2r.at[k - 1],
            device_id=along_z(k), device_id_type=MESH)

    def p3(k):
        return pltpu.make_async_remote_copy(
            esend.at[k - 1], ebuf.at[y], p3s.at[k - 1], p3r.at[k - 1],
            device_id=along_y(k), device_id_type=MESH)

    def p3_in(k):
        return pltpu.make_async_remote_copy(
            esend.at[k - 1], ebuf.at[lax.rem(y - k + ROW, ROW)], p3s.at[k - 1], p3r.at[k - 1],
            device_id=along_y(k), device_id_type=MESH)

    def ss(k):
        return pltpu.make_async_remote_copy(
            ssb, ssr.at[k - 1], sss.at[k - 1], ssrs.at[k - 1],
            device_id=along_h(k), device_id_type=MESH)

    rowbase = z * (ROW * T)
    owners = [y] + [lax.rem(y - k + ROW, ROW) for k in (1, 2, 3)]

    def last_of(j):
        return rowbase + (j + 1) * T - 1

    def gathered(s):
        return [lbuf[y, s].astype(f32)] + [xbuf[k - 1, s].astype(f32) for k in (1, 2, 3)]

    def row_sum():
        keep = []
        for s in range(2):
            begin = begin_of(s, last_of(ROW - 1))
            keep.append([begin <= last_of(j) for j in owners])
        for k in (1, 2, 3):
            p1(k).wait_recv()
        for s in range(2):
            total = jnp.zeros((PIECE, HEAD), f32)
            for part, on in zip(gathered(s), keep[s]):
                total = total + jnp.where(on, part, 0.0)
            rsend[s] = total.astype(bf16)
        for k in (2, 1):
            p2(k).start()
        for k in (1, 2, 3, 0):
            target = lax.rem(y + k, ROW)
            for s in range(2):
                begin = begin_of(s, rowbase + target * T)
                total = jnp.zeros((PIECE, HEAD), f32)
                for part, j in zip(gathered(s), owners):
                    reach = jnp.where(j < target, last_of(j), -1)
                    total = total + jnp.where(begin <= reach, part, 0.0)
                inrow[k, s] = total

    def entering():
        reach = {}
        for k in range(4):
            target = lax.rem(y + k, ROW)
            for s in range(2):
                begin = begin_of(s, rowbase + target * T)
                reach[k, s] = (begin < rowbase, begin < rowbase - ROW * T)
        for k in (1, 2):
            p2(k).wait_recv()
        for k in (2, 1, 3, 0):
            for s in range(2):
                near, far = reach[k, s]
                total = inrow[k, s] + jnp.where(near, zbuf[0, s].astype(f32), 0.0)
                total = (total + jnp.where(far, zbuf[1, s].astype(f32), 0.0)).astype(bf16)
                if k:
                    esend[k - 1, s] = total
                else:
                    ebuf[y, s] = total
            if k:
                p3(k).start()

    def attend(s, h):
        g = 2 * s + h
        for c in range(C):
            rows = slice(c * CHUNK, (c + 1) * CHUNK)
            q = qk[s, rows, :]
            first = jnp.concatenate([loc[s, rows, :]] * (CHUNK // 128), axis=1)
            cols = iota((CHUNK, CHUNK), 1)
            parts = []
            for b in range(c + 1):
                u = nn(q, kk[g, :, b * CHUNK:(b + 1) * CHUNK])
                u = u * u + 0.0625
                keep = cols + b * CHUNK >= first
                if b == c:
                    keep = keep & (cols <= iota((CHUNK, CHUNK), 0))
                parts.append(jnp.where(keep, u, 0.0).astype(bf16))
            weights = parts[0] if c == 0 else jnp.concatenate(parts, axis=1)
            nd[g, rows, :] = nt(weights, vv[g, :, :(c + 1) * CHUNK])

    def queries(s, h):
        g = 2 * s + h
        for c in range(C):
            rows = slice(c * CHUNK, (c + 1) * CHUNK)
            ab = nn(qk[s, rows, :], eq[h])
            phq[g, rows, :] = (ab[:, :256] * ab[:, 256:]).astype(bf16)

    def turn(s):
        for r0 in range(0, T, 64):
            loc[s, r0:r0 + 64, :] = places(s, base + r0 + iota((64, 128), 0))
        same = jnp.where(iota((CHUNK, CHUNK), 0) == iota((CHUNK, CHUNK), 1), 1.0, 0.0).astype(bf16)
        for c in range(C):
            rows = slice(c * CHUNK, (c + 1) * CHUNK)
            qk[s, rows, :] = nt(same, qkt[s, :, rows]).astype(bf16)
        for h in range(2):
            kk[2 * s + h] = nn(mk[h], qkt[s]).astype(bf16)

    def entered():
        for k in (1, 2, 3):
            p3_in(k).wait_recv()

    def finish(s):
        rhs = []
        f, l = iota((KEPT, HEAD), 0), iota((KEPT, HEAD), 1)
        for h in range(2):
            state = jnp.concatenate([ebuf[2 * h, s], ebuf[2 * h + 1, s]], axis=0)
            wide = state.astype(f32)
            n0, n1 = wide[ZROW:ZROW + 1], wide[ZROW + 1:ZROW + 2]
            norm = jnp.sum(jnp.where(f == l, n0, 0.0) + jnp.where(f == l + HEAD, n1, 0.0), axis=1, keepdims=True)
            norm = jnp.broadcast_to(norm, (KEPT, HEAD)).astype(bf16)
            both = jnp.concatenate([state, norm], axis=1)
            rhs.append(jnp.concatenate([both, jnp.zeros((256 - KEPT, 256), bf16)], axis=0))
        eye = iota((128, 128), 0) == iota((128, 128), 1)
        for r0 in range(0, T, 128):
            rows = slice(r0, r0 + 128)
            use = loc[s, rows, :] < 0
            squares = jnp.zeros((128, 128), f32)
            for h in range(2):
                g = 2 * s + h
                came = nn(phq[g, rows, :], rhs[h])
                num = nd[g, rows, :HEAD] + jnp.where(use, came[:, :HEAD], 0.0)
                den = nd[g, rows, HEAD:] + jnp.where(use, came[:, HEAD:], 0.0)
                a = num / den
                att[s, rows, h * HEAD:(h + 1) * HEAD] = a
                squares = squares + a * a
            col = jnp.sum(squares, axis=1, keepdims=True)
            i = r0 // 128
            ssb[s, i:i + 1, :] = jnp.sum(jnp.where(eye, col, 0.0), axis=0, keepdims=True)

    peers = sorted(range(1, hn), key=lambda k: -min(k, hn - k))

    def squares_out():
        for k in peers:
            ss(k).start()

    def scale():
        for k in peers:
            ss(k).wait_recv()
        total = ssb[...]
        for k in range(1, hn):
            total = total + ssr[k - 1]
        fac[...] = lax.rsqrt(total / (hn * 2 * HEAD) + 1e-06)

    def greet():
        pl.semaphore_wait(barrier, len(sources))

    def pieces_out():
        for k in (2, 1, 3):
            p1(k).start()

    def drain():
        rim.wait_send()
        for k in (1, 2, 3):
            p1(k).wait_send()
            p3(k).wait_send()
        for k in (1, 2):
            p2(k).wait_send()
        for k in peers:
            ss(k).wait_send()

    L = C - 1
    plan = [(bounds,), (prepare,), (columns_in,)] + [(request, 0, c) for c in range(L)]
    plan += [(arrive, 0, L), (arrive, 1, L)] + [(request, 1, c) for c in range(L)] + [(tables_in,)]
    plan += [(project, 0, L, C), (project, 1, L, C), (greet,), (rim.start,)]
    plan += [(arrive, 0, c) for c in range(L)] + [(project, 0, 0, L)]
    plan += [(arrive, 1, c) for c in range(L)] + [(project, 1, 0, L)]
    cuts = [128] + [c * CHUNK for c in range(1, C + 1)]
    for s in range(2):
        plan += [(mix, s, low, high) for low, high in zip(cuts, cuts[1:])] + [(summarise, s, 128, T)]
    plan += [(rim_in,), (mix, 0, 0, 128), (mix, 1, 0, 128)]
    plan += [(summarise, 0, 0, 128), (summarise, 1, 0, 128), (pieces_out,)]
    plan += [(ready,), (turn, 0), (turn, 1), (attend, 0, 0), (row_sum,), (attend, 0, 1), (attend, 1, 0), (entering,)]
    plan += [(queries, s, h) for s in range(2) for h in range(2)] + [(attend, 1, 1), (entered,)]
    plan += [(finish, 0), (finish, 1), (squares_out,), (scale,), (drain,)]
    for step, *where in plan:
        step(*where)


def rescale(att, fac, gain, out, obuf, osem):
    T = att.shape[1]
    eye = iota((128, 128), 0) == iota((128, 128), 1)
    g = gain[...].astype(f32).reshape(1, 2 * HEAD)

    def write(s, c):
        rows = pl.ds(c * CHUNK, CHUNK)
        return pltpu.make_async_copy(obuf.at[s, rows], out.at[s, rows], osem.at[s, c])

    for s in range(2):
        for r0 in range(0, T, 128):
            i = r0 // 128
            rows = slice(r0, r0 + 128)
            col = jnp.sum(jnp.where(eye, fac[s, i:i + 1, :], 0.0), axis=1, keepdims=True)
            obuf[s, rows, :] = (att[s, rows, :] * col * g).astype(bf16)
            if (r0 + 128) % CHUNK == 0:
                write(s, r0 // CHUNK).start()
    for s in range(2):
        for c in range(T // CHUNK):
            write(s, c).wait()


def shards(zn, hn, hidden, w_qkv, conv_weight, norm_gain, repo_lengths):
    seqs, T, D = hidden.shape
    C = T // CHUNK
    query, move = tables()
    any_spec = pl.BlockSpec(memory_space=pl.ANY)
    vmem = pl.BlockSpec(memory_space=pltpu.VMEM)
    dma = pltpu.SemaphoreType.DMA

    def pin(x):
        return pltpu.with_memory_space_constraint(jnp.asarray(x), pltpu.HBM)

    att, fac = pl.pallas_call(
        functools.partial(kernel, zn, hn),
        out_shape=(jax.ShapeDtypeStruct((seqs, T, 2 * HEAD), f32), jax.ShapeDtypeStruct((seqs, T // 128, 128), f32)),
        in_specs=[any_spec] * 6,
        out_specs=(vmem, vmem),
        scratch_shapes=[
            pltpu.VMEM((2, T, D), bf16),
            pltpu.VMEM((2 * WIDTH, D), bf16),
            pltpu.VMEM(conv_weight.shape, f32),
            pltpu.SMEM(repo_lengths.shape, jnp.int32),
            pltpu.VMEM(query.shape, bf16),
            pltpu.VMEM(move.shape, bf16),
            pltpu.VMEM((3, 2 * WIDTH, 128), f32),
            pltpu.VMEM((4, 2 * FEAT, T), f32),
            pltpu.VMEM((4, KEPT, 256), f32),
            pltpu.VMEM((2, 2 * WIDTH, 128 + T), f32),
            pltpu.VMEM((2, 8, T), jnp.int32),
            pltpu.VMEM((2, T, 128), jnp.int32),
            pltpu.VMEM((2, 128, T), bf16),
            pltpu.VMEM((2, T, 128), bf16),
            pltpu.VMEM((4, 128, T), bf16),
            pltpu.VMEM((4, 256, T), bf16),
            pltpu.VMEM((4, T, 256), bf16),
            pltpu.VMEM((4, T, 256), f32),
            pltpu.VMEM((2, RIM, 2 * WIDTH), bf16),
            pltpu.VMEM((2, RIM, 2 * WIDTH), bf16),
            pltpu.VMEM((ROW, 2, PIECE, HEAD), bf16),
            pltpu.VMEM((3, 2, PIECE, HEAD), bf16),
            pltpu.VMEM((2, PIECE, HEAD), bf16),
            pltpu.VMEM((2, 2, PIECE, HEAD), bf16),
            pltpu.VMEM((3, 2, PIECE, HEAD), bf16),
            pltpu.VMEM((ROW, 2, PIECE, HEAD), bf16),
            pltpu.VMEM((4, 2, PIECE, HEAD), f32),
            pltpu.VMEM((2, T // 128, 128), f32),
            pltpu.VMEM((hn - 1, 2, T // 128, 128), f32),
            dma,
            dma((4,)),
            dma((2, C)),
            dma((2,)),
            dma((3,)),
            dma((3,)),
            dma((2,)),
            dma((2,)),
            dma((3,)),
            dma((3,)),
            dma((hn - 1,)),
            dma((hn - 1,)),
        ],
        compiler_params=pltpu.CompilerParams(
            collective_id=0, has_side_effects=True, vmem_limit_bytes=44 * 1024 * 1024),
        name="packed_linear_attention",
    )(pin(hidden), pin(w_qkv.T), pin(conv_weight), pin(repo_lengths), pin(query), pin(move))
    return pl.pallas_call(
        rescale,
        out_shape=jax.ShapeDtypeStruct((seqs, T, 2 * HEAD), bf16),
        in_specs=[vmem, vmem, vmem],
        out_specs=any_spec,
        scratch_shapes=[pltpu.VMEM((2, T, 2 * HEAD), bf16), dma((2, C))],
        compiler_params=pltpu.CompilerParams(vmem_limit_bytes=8 * 1024 * 1024),
        name="rescale_rows",
    )(att, fac, norm_gain)


def solution(mesh):
    zn, hn = mesh.shape["seq"] // ROW, mesh.shape["head"]
    in_specs = (P(None, "seq", None), P(None, "head"), P(None, "head"), P("head"), P())
    out_specs = P(None, "seq", "head")
    return jax.shard_map(
        functools.partial(shards, zn, hn), mesh=mesh, in_specs=in_specs, out_specs=out_specs, check_vma=False)
```

```python
import functools
import jax
import jax.numpy as jnp
import numpy as np
from jax import lax
from jax.experimental import pallas as pl
from jax.experimental.pallas import tpu as pltpu
from jax.sharding import PartitionSpec as P

FEAT = 16
HEAD = 128
WIDTH = 2 * FEAT + HEAD
NSEG = 12
ROW = 4
CHUNK = 256
RIM = 16
KEPT = 160
PIECE = 80
ONE = 64
QUAD = 136
ZROW = 137
LINEAR = 144
MESH = pl.DeviceIdType.MESH
bf16 = jnp.bfloat16
f32 = jnp.float32


def tables():
    query = np.zeros((2, 128, 512), np.float32)
    move = np.zeros((2, 128, 128), np.float32)
    for h in range(2):
        qb, kb = 32 * h, 32 * h + FEAT
        for f in range(QUAD):
            d, i = f // FEAT, f % FEAT
            query[h, qb + i, f] = 1 / 8 if d else 1 / 16
            query[h, qb + (i + d) % FEAT, 256 + f] = 1.0
        query[h, ONE, QUAD] = 1.0
        query[h, ONE, 256 + QUAD] = 1.0
        for i in range(FEAT):
            query[h, qb + i, LINEAR + i] = 1 / 4
            query[h, ONE, 256 + LINEAR + i] = 1.0
            move[h, qb + i, kb + i] = 1 / 16
        move[h, ONE, ONE] = 1 / 4
    return query.astype(jnp.bfloat16), move.astype(jnp.bfloat16)


def nt(a, b):
    return lax.dot_general(a, b, (((1,), (1,)), ((), ())), preferred_element_type=f32)


def nn(a, b):
    return jnp.dot(a, b, preferred_element_type=f32)


def iota(shape, dim):
    return lax.broadcasted_iota(jnp.int32, shape, dim)


def kernel(zn, hn, hid, wq, conv_in, lengths_in, eq_in, mk_in, att, fac,
           hbuf, wbuf, conv, lengths, eq, mk, taps, kd, partial, qkv, lor, loc, qkt, qk, kk, vv, phq, nd, rim_s, rim_r, lbuf, xbuf,
           rsend, zbuf, esend, ebuf, inrow, ssb, ssr,
           wsem, csem, hsem, rim_sem, p1s, p1r, p2s, p2r, p3s, p3r, sss, ssrs):
    T = hbuf.shape[1]
    C = T // CHUNK
    G = T // 128
    me = lax.axis_index("seq")
    hd = lax.axis_index("head")
    z = me // ROW
    y = lax.rem(me, ROW)

    def at_seq(i):
        return (i, hd)

    def along_y(k):
        return (z * ROW + lax.rem(y + k + ROW, ROW), hd)

    def along_z(k):
        return (lax.rem(z + k + zn, zn) * ROW + y, hd)

    def along_h(k):
        return (me, lax.rem(hd + k + hn, hn))

    nxt = at_seq(lax.rem(me + 1, zn * ROW))
    prv = at_seq(lax.rem(me + zn * ROW - 1, zn * ROW))

    wcopy = pltpu.make_async_copy(wq, wbuf, wsem)

    def small(i):
        source, target = ((lengths_in, lengths), (conv_in, conv), (mk_in, mk), (eq_in, eq))[i]
        return pltpu.make_async_copy(source, target, csem.at[i])

    small(0).start()
    small(1).start()
    wcopy.start()
    def fetch(s, c):
        rows = pl.ds(c * CHUNK, CHUNK)
        return pltpu.make_async_copy(hid.at[s, rows], hbuf.at[s, rows], hsem.at[s, c])

    def request(s, c):
        fetch(s, c).start()

    request(0, C - 1)
    request(1, C - 1)

    barrier = pltpu.get_barrier_semaphore()
    sources = [prv] + [along_y(-k) for k in (1, 2, 3)] + [along_z(-k) for k in (1, 2)]
    sources += [along_h(-k) for k in range(1, hn)]
    for d in sources:
        pl.semaphore_signal(barrier, inc=1, device_id=d, device_id_type=MESH)

    starts = []

    def bounds():
        small(0).wait()
        for s in range(2):
            run = jnp.int32(0)
            own = []
            for r in range(NSEG - 1):
                run = run + lengths[s, r]
                own.append(run)
            starts.append(own)

    def begin_of(s, t):
        found = jnp.int32(0)
        for b in starts[s]:
            found = jnp.where(b <= t, b, found)
        return found

    base = me * T

    def places(s, pos):
        found = jnp.zeros(pos.shape, jnp.int32)
        for b in starts[s]:
            found = jnp.where(pos >= b, b, found)
        return found - base

    def prepare():
        for s in range(2):
            lor[s] = places(s, base + iota((8, T), 1))
            qkt[s, ONE:ONE + 16, :] = jnp.where(iota((16, T), 0) == 0, 1.0, 0.0).astype(bf16)
            qkt[s, ONE + 16:, :] = jnp.zeros((128 - ONE - 16, T), bf16)
            for h in range(2):
                vv[2 * s + h, HEAD:, :] = jnp.ones((HEAD, T), bf16)
        small(1).wait()
        for j in range(3):
            for c0 in range(0, 2 * WIDTH, 64):
                row = jnp.broadcast_to(conv[j:j + 1, c0:c0 + 64], (64, 64))
                eye = iota((64, 64), 0) == iota((64, 64), 1)
                col = jnp.sum(jnp.where(eye, row, 0.0), axis=1, keepdims=True)
                taps[j, c0:c0 + 64, :] = jnp.broadcast_to(col, (64, 128))

    def ready():
        for i in range(2, 4):
            small(i).wait()

    def tables_in():
        for i in range(2, 4):
            small(i).start()

    def columns_in():
        wcopy.wait()

    def arrive(s, c):
        fetch(s, c).wait()

    def project(s, low_c, high_c):
        rows = slice(low_c * CHUNK, high_c * CHUNK)
        low = nt(wbuf[...], hbuf[s, rows, :]).astype(bf16)
        qkv[s, :, 128 + low_c * CHUNK:128 + high_c * CHUNK] = low.astype(f32)
        if high_c == C:
            pick = jnp.where(iota((RIM, 128), 1) == iota((RIM, 128), 0) + 128 - RIM, 1.0, 0.0).astype(bf16)
            rim_s[s] = nt(pick, low[:, low.shape[1] - 128:]).astype(bf16)

    rim = pltpu.make_async_remote_copy(rim_s, rim_r, rim_sem.at[0], rim_sem.at[1], device_id=nxt, device_id_type=MESH)

    def rim_in():
        rim.wait_recv()
        pick = jnp.where(iota((RIM, 128), 1) == iota((RIM, 128), 0) + 128 - RIM, 1.0, 0.0).astype(bf16)
        for s in range(2):
            qkv[s, :, 0:128] = lax.dot_general(
                rim_r[s], pick, (((0,), (0,)), ((), ())), preferred_element_type=f32)

    def mix(s, low, high):
        lanes = slice(low, high)
        first = jnp.concatenate([lor[s, :, lanes]] * 4, axis=0)
        pos = low + iota((32, high - low), 1)
        one_back = first < pos
        two_back = first < pos - 1
        for r0 in range(0, 2 * WIDTH, 32):
            rows = slice(r0, r0 + 32)
            ext = qkv[s, rows, low:high + 128]
            x1 = pltpu.roll(ext, 1, 1)[:, 128:]
            x2 = pltpu.roll(ext, 2, 1)[:, 128:]

            def tap(j):
                return jnp.concatenate([taps[j, rows, :]] * ((high - low) // 128), axis=1)

            m = tap(0) * ext[:, 128:]
            m = m + tap(1) * jnp.where(one_back, x1, 0.0)
            m = m + tap(2) * jnp.where(two_back, x2, 0.0)
            m = m.astype(bf16)
            h, d = r0 // WIDTH, r0 % WIDTH
            if d == 0:
                qkt[s, 32 * h:32 * h + 32, lanes] = m
            else:
                vv[2 * s + h, d - 32:d, lanes] = m

    def summarise(s, at, until):
        inside = begin_of(s, base + T - 1) - base
        W = until - at
        lanes = slice(at, until)
        for h in range(2):
            g = 2 * s + h
            key = qkt[s, 32 * h + FEAT:32 * h + 2 * FEAT, lanes].astype(f32)
            key = jnp.where(at + iota((FEAT, W), 1) >= inside, key, 0.0)
            small_key = key * (1.0 / 16.0)
            kd[g, 0:FEAT, lanes] = small_key
            kd[g, FEAT:2 * FEAT, lanes] = small_key
            blocks = [(key * kd[g, d:d + FEAT, lanes]).astype(bf16) for d in range(8)]
            here = (at + iota((8, W), 1) >= inside) & (iota((8, W), 0) == 0)
            last = [key[:8] * kd[g, 8:16, lanes], jnp.where(here, 0.125, 0.0)]
            blocks.append(jnp.concatenate(last, axis=0).astype(bf16))
            blocks.append((key * 0.125).astype(bf16))
            total = nt(jnp.concatenate(blocks, axis=0), vv[g, :, lanes])
            if at:
                partial[g] = total
                continue
            total = partial[g] + total
            state, norm = total[:, :HEAD], total[:, HEAD:]
            f, l = iota((KEPT, HEAD), 0), iota((KEPT, HEAD), 1)
            n0 = jnp.sum(jnp.where(f == l, norm, 0.0), axis=0, keepdims=True)
            n1 = jnp.sum(jnp.where(f == l + HEAD, norm, 0.0), axis=0, keepdims=True)
            state = jnp.where(f == ZROW, n0, jnp.where(f == ZROW + 1, n1, state)).astype(bf16)
            lbuf[2 * h, s] = state[:PIECE]
            lbuf[2 * h + 1, s] = state[PIECE:]

    def p1(k):
        return pltpu.make_async_remote_copy(
            lbuf.at[lax.rem(y + k, ROW)], xbuf.at[k - 1], p1s.at[k - 1], p1r.at[k - 1],
            device_id=along_y(k), device_id_type=MESH)

    def p2(k):
        return pltpu.make_async_remote_copy(
            rsend, zbuf.at[k - 1], p2s.at[k - 1], p2r.at[k - 1],
            device_id=along_z(k), device_id_type=MESH)

    def p3(k):
        return pltpu.make_async_remote_copy(
            esend.at[k - 1], ebuf.at[y], p3s.at[k - 1], p3r.at[k - 1],
            device_id=along_y(k), device_id_type=MESH)

    def p3_in(k):
        return pltpu.make_async_remote_copy(
            esend.at[k - 1], ebuf.at[lax.rem(y - k + ROW, ROW)], p3s.at[k - 1], p3r.at[k - 1],
            device_id=along_y(k), device_id_type=MESH)

    def ss(k):
        return pltpu.make_async_remote_copy(
            ssb, ssr.at[k - 1], sss.at[k - 1], ssrs.at[k - 1],
            device_id=along_h(k), device_id_type=MESH)

    rowbase = z * (ROW * T)
    owners = [y] + [lax.rem(y - k + ROW, ROW) for k in (1, 2, 3)]

    def last_of(j):
        return rowbase + (j + 1) * T - 1

    def gathered(s):
        return [lbuf[y, s].astype(f32)] + [xbuf[k - 1, s].astype(f32) for k in (1, 2, 3)]

    def row_sum():
        keep = []
        for s in range(2):
            begin = begin_of(s, last_of(ROW - 1))
            keep.append([begin <= last_of(j) for j in owners])
        for k in (1, 2, 3):
            p1(k).wait_recv()
        for s in range(2):
            total = jnp.zeros((PIECE, HEAD), f32)
            for part, on in zip(gathered(s), keep[s]):
                total = total + jnp.where(on, part, 0.0)
            rsend[s] = total.astype(bf16)
        for k in (2, 1):
            p2(k).start()
        for k in (1, 2, 3, 0):
            target = lax.rem(y + k, ROW)
            for s in range(2):
                begin = begin_of(s, rowbase + target * T)
                total = jnp.zeros((PIECE, HEAD), f32)
                for part, j in zip(gathered(s), owners):
                    reach = jnp.where(j < target, last_of(j), -1)
                    total = total + jnp.where(begin <= reach, part, 0.0)
                inrow[k, s] = total

    def entering():
        reach = {}
        for k in range(4):
            target = lax.rem(y + k, ROW)
            for s in range(2):
                begin = begin_of(s, rowbase + target * T)
                reach[k, s] = (begin < rowbase, begin < rowbase - ROW * T)
        for k in (1, 2):
            p2(k).wait_recv()
        for k in (2, 1, 3, 0):
            for s in range(2):
                near, far = reach[k, s]
                total = inrow[k, s] + jnp.where(near, zbuf[0, s].astype(f32), 0.0)
                total = (total + jnp.where(far, zbuf[1, s].astype(f32), 0.0)).astype(bf16)
                if k:
                    esend[k - 1, s] = total
                else:
                    ebuf[y, s] = total
            if k:
                p3(k).start()

    def attend(s, h):
        g = 2 * s + h
        for c in range(C):
            rows = slice(c * CHUNK, (c + 1) * CHUNK)
            q = qk[s, rows, :]
            first = jnp.concatenate([loc[s, rows, :]] * (CHUNK // 128), axis=1)
            cols = iota((CHUNK, CHUNK), 1)
            parts = []
            for b in range(c + 1):
                u = nn(q, kk[g, :, b * CHUNK:(b + 1) * CHUNK])
                u = u * u + 0.0625
                keep = cols + b * CHUNK >= first
                if b == c:
                    keep = keep & (cols <= iota((CHUNK, CHUNK), 0))
                parts.append(jnp.where(keep, u, 0.0).astype(bf16))
            weights = parts[0] if c == 0 else jnp.concatenate(parts, axis=1)
            nd[g, rows, :] = nt(weights, vv[g, :, :(c + 1) * CHUNK])

    def queries(s, h):
        g = 2 * s + h
        for c in range(C):
            rows = slice(c * CHUNK, (c + 1) * CHUNK)
            ab = nn(qk[s, rows, :], eq[h])
            phq[g, rows, :] = (ab[:, :256] * ab[:, 256:]).astype(bf16)

    def turn(s):
        for r0 in range(0, T, 64):
            loc[s, r0:r0 + 64, :] = places(s, base + r0 + iota((64, 128), 0))
        same = jnp.where(iota((CHUNK, CHUNK), 0) == iota((CHUNK, CHUNK), 1), 1.0, 0.0).astype(bf16)
        for c in range(C):
            rows = slice(c * CHUNK, (c + 1) * CHUNK)
            qk[s, rows, :] = nt(same, qkt[s, :, rows]).astype(bf16)
        for h in range(2):
            kk[2 * s + h] = nn(mk[h], qkt[s]).astype(bf16)

    def entered():
        for k in (1, 2, 3):
            p3_in(k).wait_recv()

    def finish(s):
        rhs = []
        f, l = iota((KEPT, HEAD), 0), iota((KEPT, HEAD), 1)
        for h in range(2):
            state = jnp.concatenate([ebuf[2 * h, s], ebuf[2 * h + 1, s]], axis=0)
            wide = state.astype(f32)
            n0, n1 = wide[ZROW:ZROW + 1], wide[ZROW + 1:ZROW + 2]
            norm = jnp.sum(jnp.where(f == l, n0, 0.0) + jnp.where(f == l + HEAD, n1, 0.0), axis=1, keepdims=True)
            norm = jnp.broadcast_to(norm, (KEPT, HEAD)).astype(bf16)
            both = jnp.concatenate([state, norm], axis=1)
            rhs.append(jnp.concatenate([both, jnp.zeros((256 - KEPT, 256), bf16)], axis=0))
        eye = iota((128, 128), 0) == iota((128, 128), 1)
        for r0 in range(0, T, 128):
            rows = slice(r0, r0 + 128)
            use = loc[s, rows, :] < 0
            squares = jnp.zeros((128, 128), f32)
            for h in range(2):
                g = 2 * s + h
                came = nn(phq[g, rows, :], rhs[h])
                num = nd[g, rows, :HEAD] + jnp.where(use, came[:, :HEAD], 0.0)
                den = nd[g, rows, HEAD:] + jnp.where(use, came[:, HEAD:], 0.0)
                a = num / den
                att[s, rows, h * HEAD:(h + 1) * HEAD] = a
                squares = squares + a * a
            col = jnp.sum(squares, axis=1, keepdims=True)
            i = r0 // 128
            ssb[s, i:i + 1, :] = jnp.sum(jnp.where(eye, col, 0.0), axis=0, keepdims=True)

    peers = sorted(range(1, hn), key=lambda k: -min(k, hn - k))

    def squares_out():
        for k in peers:
            ss(k).start()

    def scale():
        for k in peers:
            ss(k).wait_recv()
        total = ssb[...]
        for k in range(1, hn):
            total = total + ssr[k - 1]
        fac[...] = lax.rsqrt(total / (hn * 2 * HEAD) + 1e-06)

    def greet():
        pl.semaphore_wait(barrier, len(sources))

    def pieces_out():
        for k in (2, 1, 3):
            p1(k).start()

    def drain():
        rim.wait_send()
        for k in (1, 2, 3):
            p1(k).wait_send()
            p3(k).wait_send()
        for k in (1, 2):
            p2(k).wait_send()
        for k in peers:
            ss(k).wait_send()

    L = C - 1
    plan = [(bounds,), (prepare,), (columns_in,)] + [(request, 0, c) for c in range(L)]
    plan += [(arrive, 0, L), (arrive, 1, L)] + [(request, 1, c) for c in range(L)] + [(tables_in,)]
    plan += [(project, 0, L, C), (project, 1, L, C), (greet,), (rim.start,)]
    plan += [(arrive, 0, c) for c in range(L)] + [(project, 0, 0, L)]
    plan += [(arrive, 1, c) for c in range(L)] + [(project, 1, 0, L)]
    cuts = [128] + [c * CHUNK for c in range(1, C + 1)]
    for s in range(2):
        plan += [(mix, s, low, high) for low, high in zip(cuts, cuts[1:])] + [(summarise, s, 128, T)]
    plan += [(rim_in,), (mix, 0, 0, 128), (mix, 1, 0, 128)]
    plan += [(summarise, 0, 0, 128), (summarise, 1, 0, 128), (pieces_out,)]
    plan += [(ready,), (turn, 0), (turn, 1), (row_sum,), (attend, 0, 0), (attend, 0, 1), (entering,), (attend, 1, 0)]
    plan += [(queries, s, h) for s in range(2) for h in range(2)] + [(attend, 1, 1), (entered,)]
    plan += [(finish, 0), (finish, 1), (squares_out,), (scale,), (drain,)]
    for step, *where in plan:
        step(*where)


def rescale(att, fac, gain, out, obuf, osem):
    T = att.shape[1]
    eye = iota((128, 128), 0) == iota((128, 128), 1)
    g = gain[...].astype(f32).reshape(1, 2 * HEAD)

    def write(s, c):
        rows = pl.ds(c * CHUNK, CHUNK)
        return pltpu.make_async_copy(obuf.at[s, rows], out.at[s, rows], osem.at[s, c])

    for s in range(2):
        for r0 in range(0, T, 128):
            i = r0 // 128
            rows = slice(r0, r0 + 128)
            col = jnp.sum(jnp.where(eye, fac[s, i:i + 1, :], 0.0), axis=1, keepdims=True)
            obuf[s, rows, :] = (att[s, rows, :] * col * g).astype(bf16)
            if (r0 + 128) % CHUNK == 0:
                write(s, r0 // CHUNK).start()
    for s in range(2):
        for c in range(T // CHUNK):
            write(s, c).wait()


def shards(zn, hn, hidden, w_qkv, conv_weight, norm_gain, repo_lengths):
    seqs, T, D = hidden.shape
    C = T // CHUNK
    query, move = tables()
    any_spec = pl.BlockSpec(memory_space=pl.ANY)
    vmem = pl.BlockSpec(memory_space=pltpu.VMEM)
    dma = pltpu.SemaphoreType.DMA

    def pin(x):
        return pltpu.with_memory_space_constraint(jnp.asarray(x), pltpu.HBM)

    att, fac = pl.pallas_call(
        functools.partial(kernel, zn, hn),
        out_shape=(jax.ShapeDtypeStruct((seqs, T, 2 * HEAD), f32), jax.ShapeDtypeStruct((seqs, T // 128, 128), f32)),
        in_specs=[any_spec] * 6,
        out_specs=(vmem, vmem),
        scratch_shapes=[
            pltpu.VMEM((2, T, D), bf16),
            pltpu.VMEM((2 * WIDTH, D), bf16),
            pltpu.VMEM(conv_weight.shape, f32),
            pltpu.SMEM(repo_lengths.shape, jnp.int32),
            pltpu.VMEM(query.shape, bf16),
            pltpu.VMEM(move.shape, bf16),
            pltpu.VMEM((3, 2 * WIDTH, 128), f32),
            pltpu.VMEM((4, 2 * FEAT, T), f32),
            pltpu.VMEM((4, KEPT, 256), f32),
            pltpu.VMEM((2, 2 * WIDTH, 128 + T), f32),
            pltpu.VMEM((2, 8, T), jnp.int32),
            pltpu.VMEM((2, T, 128), jnp.int32),
            pltpu.VMEM((2, 128, T), bf16),
            pltpu.VMEM((2, T, 128), bf16),
            pltpu.VMEM((4, 128, T), bf16),
            pltpu.VMEM((4, 256, T), bf16),
            pltpu.VMEM((4, T, 256), bf16),
            pltpu.VMEM((4, T, 256), f32),
            pltpu.VMEM((2, RIM, 2 * WIDTH), bf16),
            pltpu.VMEM((2, RIM, 2 * WIDTH), bf16),
            pltpu.VMEM((ROW, 2, PIECE, HEAD), bf16),
            pltpu.VMEM((3, 2, PIECE, HEAD), bf16),
            pltpu.VMEM((2, PIECE, HEAD), bf16),
            pltpu.VMEM((2, 2, PIECE, HEAD), bf16),
            pltpu.VMEM((3, 2, PIECE, HEAD), bf16),
            pltpu.VMEM((ROW, 2, PIECE, HEAD), bf16),
            pltpu.VMEM((4, 2, PIECE, HEAD), f32),
            pltpu.VMEM((2, T // 128, 128), f32),
            pltpu.VMEM((hn - 1, 2, T // 128, 128), f32),
            dma,
            dma((4,)),
            dma((2, C)),
            dma((2,)),
            dma((3,)),
            dma((3,)),
            dma((2,)),
            dma((2,)),
            dma((3,)),
            dma((3,)),
            dma((hn - 1,)),
            dma((hn - 1,)),
        ],
        compiler_params=pltpu.CompilerParams(
            collective_id=0, has_side_effects=True, vmem_limit_bytes=44 * 1024 * 1024),
        name="packed_linear_attention",
    )(pin(hidden), pin(w_qkv.T), pin(conv_weight), pin(repo_lengths), pin(query), pin(move))
    return pl.pallas_call(
        rescale,
        out_shape=jax.ShapeDtypeStruct((seqs, T, 2 * HEAD), bf16),
        in_specs=[vmem, vmem, vmem],
        out_specs=any_spec,
        scratch_shapes=[pltpu.VMEM((2, T, 2 * HEAD), bf16), dma((2, C))],
        compiler_params=pltpu.CompilerParams(vmem_limit_bytes=8 * 1024 * 1024),
        name="rescale_rows",
    )(att, fac, norm_gain)


def solution(mesh):
    zn, hn = mesh.shape["seq"] // ROW, mesh.shape["head"]
    in_specs = (P(None, "seq", None), P(None, "head"), P(None, "head"), P("head"), P())
    out_specs = P(None, "seq", "head")
    return jax.shard_map(
        functools.partial(shards, zn, hn), mesh=mesh, in_specs=in_specs, out_specs=out_specs, check_vma=False)
```
